32 devices in a mesh: tm: 8 (over z, x), space: 4 (over y, core).
Axes of the slice: x: 2, y: 2, z: 4, core: 2. Of those that a mesh axis runs over, the one named last changes fastest.
Arguments:
- latent: bfloat16 [2, 8, 512, 1152], P(None, 'tm', 'space'), may hold values from -6 to 6
- spatial_cache: bfloat16 [2, 8, 512, 1152], P(None, 'tm', 'space'), may hold values from -6 to 6
- modulation: float32 [2, 2, 3, 1152], replicated, may hold values from -3 to 3
- weights: bfloat16 [2, 1152, 4608], P(None, 'tm'), may hold values from -0.1875 to 0.1875
Outputs:
- block_out: bfloat16 [2, 8, 512, 1152], P(None, 'tm', 'space')
- new_spatial: bfloat16 [2, 8, 512, 1152], P(None, 'tm', 'space')
- new_temporal: bfloat16 [2, 8, 512, 1152], P(None, 'tm', 'space')
The draws below stay inside these ranges and needn't reach their ends.
All inputs are finite; a program needn't handle non-finite values.
Results may differ from the reference program's by a relative error of at most 0.015.
Values may be sent and summed in bfloat16 or wider, within the bound.
A program may use at most 128 MiB of HBM per device.

```python
import jax
import jax.numpy as jnp
from jax import lax

D = 1152
HEADS = 16
HEAD_DIM = 72
BATCH = 2
FRAMES = 8
SPAN = 512


def levels(key, dims, split, least, largest):
    factor_of, own = 1.0, jax.random.fold_in(key, 6)
    for dim, blocks in split:
        steps = jnp.exp(jax.random.uniform(jax.random.fold_in(own, dim), (blocks,), jnp.float32, least / len(split), largest / len(split)))
        factor_of = factor_of * jnp.repeat(steps, dims[dim] // blocks).reshape([-1 if axis == dim else 1 for axis in range(len(dims))])
    return factor_of


def gaussian(own_key, shape, width, limit, pieces=(), kind=jnp.bfloat16):
    result = jax.random.normal(own_key, shape, jnp.float32) * width
    if len(pieces) > 0:
        result = levels(own_key, shape, pieces, -0.22, 0.18) * result
    return jnp.clip(result, min=-limit, max=limit).astype(kind)


def setup_inputs(seed: int = 0) -> dict:
    streams_of = jax.random.split(jax.random.key(seed), 5)
    latent = gaussian(streams_of[0], (BATCH, FRAMES, SPAN, D), 1.0, 6.0, ((1, 8), (2, 4)))
    spatial_cache = gaussian(streams_of[1], (BATCH, FRAMES, SPAN, D), 1.0, 6.0, ((1, 8), (2, 4)))
    modulation = gaussian(streams_of[2], (2, 2, 3, D), 0.5, 3.0, (), jnp.float32)
    weights = gaussian(streams_of[3], (2, D, 4 * D), D ** -0.5, 0.1875, ((1, 8),))
    return dict(latent=latent, spatial_cache=spatial_cache, modulation=modulation, weights=weights)


def layer_norm(h):
    x = h.astype(jnp.float32)
    mean = lax.optimization_barrier(jnp.mean(x, axis=-1, keepdims=True))
    var = lax.optimization_barrier(jnp.mean((x - mean) ** 2, axis=-1, keepdims=True))
    return (x - mean) * lax.rsqrt(var + 1e-06)

def modulate(h, mods):
    return (layer_norm(h) * (1.0 + mods[1]) + mods[0]).astype(jnp.bfloat16)

def rms_norm(v):
    return v * lax.rsqrt(lax.optimization_barrier(jnp.mean(v * v, axis=-1, keepdims=True)) + 1e-06)

def attend(query, keys, values):
    scores = jnp.einsum('nlhd,nmhd->nhlm', query.astype(jnp.float32), keys.astype(jnp.float32)) / jnp.sqrt(jnp.float32(HEAD_DIM))
    expo = jnp.exp(scores)
    probs = (expo / lax.optimization_barrier(jnp.sum(expo, axis=-1, keepdims=True))).astype(jnp.bfloat16)
    out = jnp.einsum('nhlm,nmhd->nlhd', probs.astype(jnp.float32), values.astype(jnp.float32))
    return out.astype(jnp.bfloat16)

def fresh_attention(h, mods, weight, spatial):
    modin = modulate(h, mods)
    flat = modin.reshape(-1, D)
    qkv = jnp.dot(flat, weight[:, :3 * D], preferred_element_type=jnp.float32)
    qkv = qkv.reshape(BATCH, FRAMES, SPAN, HEADS, 3, HEAD_DIM)
    query = rms_norm(qkv[..., 0, :]).astype(jnp.bfloat16)
    keys = rms_norm(qkv[..., 1, :]).astype(jnp.bfloat16)
    values = qkv[..., 2, :].astype(jnp.bfloat16)
    if spatial:
        shape = (BATCH * FRAMES, 1, SPAN, HEADS, HEAD_DIM)
        items = (query.reshape(shape), keys.reshape(shape), values.reshape(shape))
        out = lax.map(lambda t: attend(t[0], t[1], t[2]), items)
        out = out.reshape(BATCH, FRAMES, SPAN, D)
    else:

        def tokens_major(t):
            return jnp.transpose(t, (0, 2, 1, 3, 4)).reshape(BATCH * SPAN, FRAMES, HEADS, HEAD_DIM)
        out = attend(tokens_major(query), tokens_major(keys), tokens_major(values))
        out = jnp.transpose(out.reshape(BATCH, SPAN, FRAMES, D), (0, 2, 1, 3))
    proj = jnp.dot(out.reshape(-1, D), weight[:, 3 * D:], preferred_element_type=jnp.float32)
    return proj.astype(jnp.bfloat16).reshape(BATCH, FRAMES, SPAN, D)

def add_gated(h, gate, branch):
    return (h.astype(jnp.float32) + gate * branch.astype(jnp.float32)).astype(jnp.bfloat16)

def reference(latent, spatial_cache, modulation, weights):
    h = add_gated(latent, modulation[0, 0, 2], spatial_cache)
    new_temporal = fresh_attention(h, modulation[0, 1], weights[1], False)
    h = add_gated(h, modulation[0, 1, 2], new_temporal)
    new_spatial = fresh_attention(h, modulation[1, 0], weights[0], True)
    h = add_gated(h, modulation[1, 0, 2], new_spatial)
    block_out = add_gated(h, modulation[1, 1, 2], new_temporal)
    return (block_out, new_spatial, new_temporal)
```

```python
import functools

import jax
import jax.numpy as jnp
from jax import lax
from jax.experimental import pallas as pl
from jax.experimental.pallas import tpu as pltpu
from jax.sharding import PartitionSpec as P

D = 1152
HEADS = 16
HEAD_DIM = 72
MESH = pl.DeviceIdType.MESH
VMEM = pltpu.VMEM
LIMIT = 56 * 1024 * 1024


def add_gated(h, gate, branch):
    return (h.astype(jnp.float32) + gate * branch.astype(jnp.float32)).astype(jnp.bfloat16)


def modulate(h, shift, scale):
    x = h.astype(jnp.float32)
    mean = jnp.mean(x, axis=-1, keepdims=True)
    c = x - mean
    var = jnp.mean(c * c, axis=-1, keepdims=True)
    return (c * lax.rsqrt(var + 1e-06) * (1.0 + scale) + shift).astype(jnp.bfloat16)


def mod_row(mod_ref, step, attn, which):
    row = (step * 2 + attn) * 3 + which
    return mod_ref[row : row + 1, :]


def place():
    return lax.axis_index("tm"), lax.axis_index("space")


def device(t, s):
    return {"tm": t, "space": s}


def greet(peers):
    barrier = pltpu.get_barrier_semaphore()
    for t, s in peers:
        pl.semaphore_signal(barrier, inc=1, device_id=device(t, s), device_id_type=MESH)
    pl.semaphore_wait(barrier, len(peers))


def tm_peers(nt, t, s):
    return [(lax.rem(t + k, nt), s) for k in range(1, nt)]


def space_peers(ns, t, s):
    return [(t, lax.rem(s + k, ns)) for k in range(1, ns)]


def chip_peers(ns, s):
    return [lax.rem(s + 2 * k, ns) for k in range(1, ns // 2)], s + 1 - 2 * lax.rem(s, 2)


def remote(src, dst, send, recv, t, s):
    return pltpu.make_async_remote_copy(
        src_ref=src, dst_ref=dst, send_sem=send, recv_sem=recv, device_id=device(t, s), device_id_type=MESH
    )


def spread(slots, send, recv, ns, t, s, chunks, ready):
    others, sib = chip_peers(ns, s)
    started = []
    for n, i in enumerate(chunks):
        ready(i)
        for k, o in enumerate(others):
            c = remote(slots.at[s, i], slots.at[s, i], send.at[k, n], recv.at[s, i], t, o)
            c.start()
            started.append(c)
        c = remote(slots.at[s, i], slots.at[s, i], send.at[len(others), n], recv.at[s, i], t, sib)
        c.start()
        started.append(c)
    for n, i in enumerate(chunks):
        for k, o in enumerate(others):
            got = remote(slots.at[o, i], slots.at[o, i], send.at[0, 0], recv.at[o, i], t, sib)
            got.wait_recv()
            c = remote(slots.at[o, i], slots.at[o, i], send.at[len(others) + 1 + k, n], recv.at[o, i], t, sib)
            c.start()
            started.append(c)
    for n, i in enumerate(chunks):
        for base in [sib] + [o + sib - s for o in others]:
            remote(slots.at[base, i], slots.at[base, i], send.at[0, 0], recv.at[base, i], t, sib).wait_recv()
    return started


def enter_kernel(nt, ns, lat, cache, mod, x, h_out, own, send_a, send_b, recv):
    t, s = place()
    greet(tm_peers(nt, t, s) + space_peers(ns, t, s))
    h = add_gated(lat[...], mod_row(mod, 0, 0, 2), cache[...])
    h_out[...] = h
    own[...] = modulate(h, mod_row(mod, 0, 1, 0), mod_row(mod, 0, 1, 1)).reshape(own.shape)
    started = []
    for k in range(1, nt):
        p = lax.rem(t + k, nt)
        c = remote(own.at[p], x.at[s, t], send_a.at[k], recv.at[s, t], p, s)
        c.start()
        started.append(c)
    x[s, t] = own[t]

    order = [t] + [lax.rem(t + nt - k, nt) for k in range(1, nt)]

    def ready(q):
        if q is not t:
            remote(own.at[0], x.at[s, q], send_a.at[0], recv.at[s, q], t, s).wait_recv()

    started += spread(x, send_b, recv, ns, t, s, order, ready)
    for c in started:
        c.wait_send()


def heads_of(qkv, heads):
    out = []
    for i in range(heads):
        parts = [qkv[:, (3 * i + j) * HEAD_DIM : (3 * i + j + 1) * HEAD_DIM] for j in range(3)]
        for j in range(2):
            sq = jnp.sum(parts[j] * parts[j], axis=-1, keepdims=True)
            parts[j] = parts[j] * lax.rsqrt(sq * (1.0 / HEAD_DIM) + 1e-06)
        out.append([p.astype(jnp.bfloat16) for p in parts])
    return out


def attend(q, k, v, mask):
    scores = lax.dot_general(q, k, (((1,), (1,)), ((), ())), preferred_element_type=jnp.float32)
    expo = jnp.exp(scores * (HEAD_DIM**-0.5))
    if mask is not None:
        expo = jnp.where(mask, expo, 0.0)
    probs = (expo / jnp.sum(expo, axis=-1, keepdims=True)).astype(jnp.bfloat16)
    return jnp.dot(probs, v, preferred_element_type=jnp.float32).astype(jnp.bfloat16)


def project(o, wo, ns):
    acc = jnp.dot(o[0], wo[0], preferred_element_type=jnp.float32)
    for i in range(1, ns):
        acc += jnp.dot(o[i], wo[i], preferred_element_type=jnp.float32)
    return acc.astype(jnp.bfloat16)


def temporal_kernel(
    nt, ns, x, wq, wo, h_ref, mod, x2, h_out, new_t, mine, o, y, back, send_o, recv_o, send_y, recv_y, send_b, recv_b
):
    t, s = place()
    greet(tm_peers(nt, t, s) + space_peers(ns, t, s))
    heads = HEADS // ns
    rows = x.shape[1]
    block = rows // nt
    mask = lax.rem(lax.broadcasted_iota(jnp.int32, (rows, rows), 0), block) == lax.rem(
        lax.broadcasted_iota(jnp.int32, (rows, rows), 1), block
    )

    def tile(step, carry):
        p = lax.rem(s + step, ns)
        qkv = jnp.dot(x[p], wq[...], preferred_element_type=jnp.float32)
        outs = [attend(q, k, v, mask) for q, k, v in heads_of(qkv, heads)]
        mine[p] = jnp.concatenate(outs, axis=-1)

        @pl.when(step < ns)
        def _():
            remote(mine.at[p], o.at[s], send_o.at[step], recv_o.at[s], t, p).start()

        return carry

    lax.fori_loop(1, ns + 1, tile, 0)
    o[s] = mine[s]
    for k in range(1, ns):
        q = lax.rem(s + k, ns)
        remote(mine.at[q], o.at[q], send_o.at[k], recv_o.at[q], t, q).wait_recv()
    y[...] = project(o, wo, ns).reshape(y.shape)
    started = []
    for k in range(1, nt):
        p = lax.rem(t + k, nt)
        c = remote(y.at[p], back.at[t], send_y.at[k], recv_y.at[t], p, s)
        c.start()
        started.append(c)
    back[t] = y[t]
    for k in range(1, nt):
        q = lax.rem(t + k, nt)
        remote(y.at[q], back.at[q], send_y.at[k], recv_y.at[q], q, s).wait_recv()
    fresh = back[...].reshape(rows, D)
    new_t[...] = fresh
    h = add_gated(h_ref[...], mod_row(mod, 0, 1, 2), fresh)
    h_out[...] = h
    x2[s] = modulate(h, mod_row(mod, 1, 0, 0), mod_row(mod, 1, 0, 1)).reshape(x2.shape[1:])
    started += spread(x2, send_b, recv_b, ns, t, s, list(range(x2.shape[1])), lambda i: None)
    for k in range(1, ns):
        q = lax.rem(s + k, ns)
        remote(mine.at[q], o.at[q], send_o.at[k], recv_o.at[q], t, q).wait_send()
    for c in started:
        c.wait_send()


def spatial_kernel(
    batch, ns, x, wq, wo, h_ref, nt_ref, mod, block_out, new_s, qs, ks, vs, mine, o, send_o, recv_o
):
    t, s = place()
    greet(space_peers(ns, t, s))
    heads = HEADS // ns
    rows = x.shape[1]
    span = rows // batch

    def proj(p, carry):
        qkv = jnp.dot(x[p], wq[...], preferred_element_type=jnp.float32)
        for i, (q, k, v) in enumerate(heads_of(qkv, heads)):
            for b in range(batch):
                part = slice(b * span, (b + 1) * span)
                qs[p, i, b] = q[part]
                ks[i, b, p] = k[part]
                vs[i, b, p] = v[part]
        return carry

    lax.fori_loop(0, ns, proj, 0)

    def tile(step, carry):
        p = lax.rem(s + step, ns)
        for b in range(batch):
            outs = []
            for i in range(heads):
                keys = ks[i, b].reshape(ns * span, HEAD_DIM)
                vals = vs[i, b].reshape(ns * span, HEAD_DIM)
                outs.append(attend(qs[p, i, b], keys, vals, None))
            mine[p, b * span : (b + 1) * span, :] = jnp.concatenate(outs, axis=-1)

        @pl.when(step < ns)
        def _():
            remote(mine.at[p], o.at[s], send_o.at[step], recv_o.at[s], t, p).start()

        return carry

    lax.fori_loop(1, ns + 1, tile, 0)
    o[s] = mine[s]
    for k in range(1, ns):
        q = lax.rem(s + k, ns)
        remote(mine.at[q], o.at[q], send_o.at[k], recv_o.at[q], t, q).wait_recv()
    fresh = project(o, wo, ns)
    new_s[...] = fresh
    h = add_gated(h_ref[...], mod_row(mod, 1, 0, 2), fresh)
    block_out[...] = add_gated(h, mod_row(mod, 1, 1, 2), nt_ref[...])
    for k in range(1, ns):
        q = lax.rem(s + k, ns)
        remote(mine.at[q], o.at[q], send_o.at[k], recv_o.at[q], t, q).wait_send()


def call(kernel, args, outs, scratch, collective_id, flops):
    return pl.pallas_call(
        kernel,
        out_shape=[jax.ShapeDtypeStruct(shape, jnp.bfloat16) for shape in outs],
        in_specs=[pl.BlockSpec(memory_space=VMEM)] * len(args),
        out_specs=[pl.BlockSpec(memory_space=VMEM)] * len(outs),
        scratch_shapes=scratch,
        cost_estimate=pl.CostEstimate(flops=flops, bytes_accessed=100_000_000, transcendentals=0),
        compiler_params=pltpu.CompilerParams(
            collective_id=collective_id, has_side_effects=True, vmem_limit_bytes=LIMIT
        ),
    )(*args)


def shards(nt, ns, latent, spatial_cache, modulation, weights):
    s = lax.axis_index("space")
    batch, _, span, _ = latent.shape
    rows = batch * span
    block = rows // nt
    wide = 3 * D // ns
    dma = pltpu.SemaphoreType.DMA
    bf16 = jnp.bfloat16
    chunks = 8

    def fetch(a):
        own = lax.dynamic_slice(weights[a], (0, s * wide), (weights.shape[1], wide))
        wq = lax.all_gather(own, "tm", axis=0, tiled=True)
        wo = lax.all_gather(weights[a][:, 3 * D :], "tm", axis=0, tiled=True)
        return wq, wo.reshape(ns, D // ns, D)

    wq_t, wo_t = fetch(1)
    wq_s, wo_s = fetch(0)
    mod = modulation.reshape(12, D)
    x, h = call(
        functools.partial(enter_kernel, nt, ns),
        (latent.reshape(rows, D), spatial_cache.reshape(rows, D), mod),
        [(ns, nt, block, D), (rows, D)],
        [VMEM((nt, block, D), bf16), dma((nt,)), dma((ns, nt)), dma((ns, nt))],
        0,
        1_000_000,
    )
    x2, h, new_t = call(
        functools.partial(temporal_kernel, nt, ns),
        (x.reshape(ns, rows, D), wq_t, wo_t, h, mod),
        [(ns, chunks, rows // chunks, D), (rows, D), (rows, D)],
        [
            VMEM((ns, rows, D // ns), bf16),
            VMEM((ns, rows, D // ns), bf16),
            VMEM((nt, block, D), bf16),
            VMEM((nt, block, D), bf16),
            dma((ns,)),
            dma((ns,)),
            dma((nt,)),
            dma((nt,)),
            dma((ns, chunks)),
            dma((ns, chunks)),
        ],
        1,
        3_000_000_000,
    )
    heads = HEADS // ns
    block_out, new_s = call(
        functools.partial(spatial_kernel, batch, ns),
        (x2.reshape(ns, rows, D), wq_s, wo_s, h, new_t, mod),
        [(rows, D), (rows, D)],
        [
            VMEM((ns, heads, batch, span, HEAD_DIM), bf16),
            VMEM((heads, batch, ns, span, HEAD_DIM), bf16),
            VMEM((heads, batch, ns, span, HEAD_DIM), bf16),
            VMEM((ns, rows, D // ns), bf16),
            VMEM((ns, rows, D // ns), bf16),
            dma((ns,)),
            dma((ns,)),
        ],
        2,
        3_000_000_000,
    )
    return tuple(a.reshape(latent.shape) for a in (block_out, new_s, new_t))


def solution(mesh):
    part = P(None, "tm", "space", None)
    return jax.shard_map(
        functools.partial(shards, mesh.shape["tm"], mesh.shape["space"]),
        mesh=mesh,
        in_specs=(part, part, P(), P(None, "tm", None)),
        out_specs=(part, part, part),
        check_vma=False,
    )
```

```python
import functools

import jax
import jax.numpy as jnp
from jax import lax
from jax.experimental import pallas as pl
from jax.experimental.pallas import tpu as pltpu
from jax.sharding import PartitionSpec as P

D = 1152
HEADS = 16
HEAD_DIM = 72
MESH = pl.DeviceIdType.MESH
VMEM = pltpu.VMEM
LIMIT = 56 * 1024 * 1024


def add_gated(h, gate, branch):
    return (h.astype(jnp.float32) + gate * branch.astype(jnp.float32)).astype(jnp.bfloat16)


def modulate(h, shift, scale):
    x = h.astype(jnp.float32)
    mean = jnp.mean(x, axis=-1, keepdims=True)
    c = x - mean
    var = jnp.mean(c * c, axis=-1, keepdims=True)
    return (c * lax.rsqrt(var + 1e-06) * (1.0 + scale) + shift).astype(jnp.bfloat16)


def mod_row(mod_ref, step, attn, which):
    row = (step * 2 + attn) * 3 + which
    return mod_ref[row : row + 1, :]


def place():
    return lax.axis_index("tm"), lax.axis_index("space")


def device(t, s):
    return {"tm": t, "space": s}


def greet(peers):
    barrier = pltpu.get_barrier_semaphore()
    for t, s in peers:
        pl.semaphore_signal(barrier, inc=1, device_id=device(t, s), device_id_type=MESH)
    pl.semaphore_wait(barrier, len(peers))


def tm_peers(nt, t, s):
    return [(lax.rem(t + k, nt), s) for k in range(1, nt)]


def space_peers(ns, t, s):
    return [(t, lax.rem(s + k, ns)) for k in range(1, ns)]


def chip_peers(ns, s):
    return [lax.rem(s + 2 * k, ns) for k in range(1, ns // 2)], s + 1 - 2 * lax.rem(s, 2)


def remote(src, dst, send, recv, t, s):
    return pltpu.make_async_remote_copy(
        src_ref=src, dst_ref=dst, send_sem=send, recv_sem=recv, device_id=device(t, s), device_id_type=MESH
    )


class Spread:
    def __init__(self, slots, send, recv, ns, t, s, chunks):
        self.slots, self.send, self.recv, self.t, self.s, self.chunks = slots, send, recv, t, s, chunks
        self.others, self.sib = chip_peers(ns, s)
        self.started = []

    def copy(self, base, i, lane, n, to):
        ref = self.slots.at[base, i]
        return remote(ref, ref, self.send.at[lane, n], self.recv.at[base, i], self.t, to)

    def push(self, base, i, lane, n, to):
        c = self.copy(base, i, lane, n, to)
        c.start()
        self.started.append(c)

    def begin(self, ready=None):
        for n, i in enumerate(self.chunks):
            if ready is not None:
                ready(i)
            for k, o in enumerate(self.others):
                self.push(self.s, i, k, n, o)
            self.push(self.s, i, len(self.others), n, self.sib)

    def forward(self):
        for n, i in enumerate(self.chunks):
            for k, o in enumerate(self.others):
                self.copy(o, i, 0, 0, self.sib).wait_recv()
                self.push(o, i, len(self.others) + 1 + k, n, self.sib)

    def finish(self):
        for i in self.chunks:
            for base in [self.sib] + [o + self.sib - self.s for o in self.others]:
                self.copy(base, i, 0, 0, self.sib).wait_recv()

    def drain(self):
        for c in self.started:
            c.wait_send()


class Gather:
    def __init__(self, slots, send, recv, nt, t, s):
        self.slots, self.send, self.recv, self.s, self.t = slots, send, recv, s, t
        self.line = nt // 2
        self.z = t // 2
        self.pair = t + 1 - 2 * lax.rem(t, 2)
        self.stage_at = 0

    def copy(self, slot, kind, to):
        ref = self.slots.at[slot]
        return remote(ref, ref, self.send.at[kind, slot], self.recv.at[slot], to, self.s)

    def each(self, d, act, arrive):
        t, z, line = self.t, self.z, self.line

        def up(slot):
            pl.when(z + 1 < line)(lambda: act(self.copy(slot, 0, t + 2)))

        def down(slot):
            pl.when(z > 0)(lambda: act(self.copy(slot, 1, t - 2)))

        if d == 0:
            up(t)
            down(t)
            act(self.copy(t, 2, self.pair))
            return

        def from_below():
            slot = t - 2 * d
            if arrive:
                self.copy(slot, 2, self.pair).wait_recv()
            up(slot)
            act(self.copy(slot, 2, self.pair))

        def from_above():
            slot = t + 2 * d
            if arrive:
                self.copy(slot, 2, self.pair).wait_recv()
            down(slot)
            act(self.copy(slot, 2, self.pair))

        pl.when(z >= d)(from_below)
        pl.when(z + d < line)(from_above)

    def stage(self):
        if self.stage_at < self.line:
            self.each(self.stage_at, lambda c: c.start(), True)
            self.stage_at += 1

    def finish(self):
        while self.stage_at < self.line:
            self.stage()
        for z in range(self.line):
            self.copy(2 * z + 1 - lax.rem(self.t, 2), 2, self.pair).wait_recv()

    def drain(self):
        for d in range(self.line):
            self.each(d, lambda c: c.wait_send(), False)


def heads_of(qkv, heads):
    out = []
    for i in range(heads):
        parts = [qkv[:, (3 * i + j) * HEAD_DIM : (3 * i + j + 1) * HEAD_DIM] for j in range(3)]
        for j in range(2):
            sq = jnp.sum(parts[j] * parts[j], axis=-1, keepdims=True)
            parts[j] = parts[j] * lax.rsqrt(sq * (1.0 / HEAD_DIM) + 1e-06)
        out.append([p.astype(jnp.bfloat16) for p in parts])
    return out


def attend(q, k, v, mask):
    scores = lax.dot_general(q, k, (((1,), (1,)), ((), ())), preferred_element_type=jnp.float32)
    expo = jnp.exp(scores * (HEAD_DIM**-0.5))
    if mask is not None:
        expo = jnp.where(mask, expo, 0.0)
    probs = (expo / jnp.sum(expo, axis=-1, keepdims=True)).astype(jnp.bfloat16)
    return jnp.dot(probs, v, preferred_element_type=jnp.float32).astype(jnp.bfloat16)


def kernel(
    nt, ns, batch, lat, cache, mod, weights, block_out, new_s, new_t,
    x, x2, own, w, wo, mine, o, y, back, qs, ks, vs,
    send_w, recv_w, send_wo, recv_wo, send_a, send_x, recv_x, send_x2, recv_x2, send_o, recv_o, send_y, recv_y,
):
    t, s = place()
    heads = HEADS // ns
    rows = x.shape[1] * x.shape[2]
    block = rows // nt
    span = rows // batch
    out_cols, in_cols = D // ns, 3 * D // ns
    depth = weights.shape[1]

    for i in range(ns):

        @pl.when(s == i)
        def _():
            for a in range(2):
                w[a, t, :, :out_cols] = weights[a, :, 3 * D + i * out_cols : 3 * D + (i + 1) * out_cols]
                w[a, t, :, out_cols:] = weights[a, :, i * in_cols : (i + 1) * in_cols]

    greet(tm_peers(nt, t, s) + space_peers(ns, t, s))
    gathers = [Gather(w.at[a], send_w.at[a], recv_w.at[a], nt, t, s) for a in range(2)]
    first, second = gathers[1], gathers[0]
    first.stage()

    def spread_out(a):
        wo[a, s] = w[a, :, :, :out_cols].reshape(wo.shape[2:])
        return Spread(wo.at[a], send_wo.at[a], recv_wo.at[a], ns, t, s, list(range(wo.shape[2])))

    h = add_gated(lat[...], mod_row(mod, 0, 0, 2), cache[...])
    block_out[...] = h
    own[...] = modulate(h, mod_row(mod, 0, 1, 0), mod_row(mod, 0, 1, 1)).reshape(own.shape)
    started = []
    for k in range(1, nt):
        p = lax.rem(t + k, nt)
        c = remote(own.at[p], x.at[s, t], send_a.at[k], recv_x.at[s, t], p, s)
        c.start()
        started.append(c)
    x[s, t] = own[t]
    first.stage()

    def ready(q):
        if q is not t:
            remote(own.at[0], x.at[s, q], send_a.at[0], recv_x.at[s, q], t, s).wait_recv()

    tokens = Spread(x, send_x, recv_x, ns, t, s, [t] + [lax.rem(t + nt - k, nt) for k in range(1, nt)])
    tokens.begin(ready)
    first.stage()
    tokens.forward()
    first.finish()
    second.stage()
    out_t = spread_out(1)
    out_t.begin()
    tokens.finish()

    mask = lax.rem(lax.broadcasted_iota(jnp.int32, (rows, rows), 0), block) == lax.rem(
        lax.broadcasted_iota(jnp.int32, (rows, rows), 1), block
    )

    def projected(a, tokens_in):
        qkv = jnp.dot(tokens_in, w[a].reshape(nt * depth, out_cols + in_cols), preferred_element_type=jnp.float32)
        return heads_of(qkv[:, out_cols:], heads)

    def send_out(a, step, p):
        return remote(mine.at[a, p], o.at[a, s], send_o.at[a, step], recv_o.at[a, s], t, p)

    def temporal_tile(step, carry):
        p = lax.rem(s + step, ns)
        outs = [attend(q, k, v, mask) for q, k, v in projected(1, x[p].reshape(rows, D))]
        mine[1, p] = jnp.concatenate(outs, axis=-1)
        pl.when(step < ns)(lambda: send_out(1, step, p).start())
        return carry

    def collect(a):
        o[a, s] = mine[a, s]
        for k in range(1, ns):
            q = lax.rem(s + k, ns)
            remote(mine.at[a, q], o.at[a, q], send_o.at[a, k], recv_o.at[a, q], t, q).wait_recv()

    def project(a):
        attn = jnp.concatenate([o[a, i] for i in range(ns)], axis=-1)
        cols = [
            jnp.dot(attn, wo[a, i].reshape(D, out_cols), preferred_element_type=jnp.float32).astype(jnp.bfloat16)
            for i in range(ns)
        ]
        return jnp.concatenate(cols, axis=-1)

    lax.fori_loop(1, ns + 1, temporal_tile, 0)
    out_t.forward()
    second.stage()
    out_t.finish()
    collect(1)
    y[...] = project(1).reshape(y.shape)
    for k in range(1, nt):
        p = lax.rem(t + k, nt)
        c = remote(y.at[p], back.at[t], send_y.at[k], recv_y.at[t], p, s)
        c.start()
        started.append(c)
    back[t] = y[t]
    second.stage()
    for k in range(1, nt):
        q = lax.rem(t + k, nt)
        remote(y.at[q], back.at[q], send_y.at[k], recv_y.at[q], q, s).wait_recv()
    fresh = back[...].reshape(rows, D)
    new_t[...] = fresh
    h = add_gated(block_out[...], mod_row(mod, 0, 1, 2), fresh)
    block_out[...] = h
    x2[s] = modulate(h, mod_row(mod, 1, 0, 0), mod_row(mod, 1, 0, 1)).reshape(x2.shape[1:])
    tokens2 = Spread(x2, send_x2, recv_x2, ns, t, s, list(range(x2.shape[1])))
    tokens2.begin()
    second.finish()
    tokens2.forward()
    out_s = spread_out(0)
    out_s.begin()
    tokens2.finish()

    def proj(p, carry):
        for i, (q, k, v) in enumerate(projected(0, x2[p].reshape(rows, D))):
            for b in range(batch):
                part = slice(b * span, (b + 1) * span)
                qs[p, i, b] = q[part]
                ks[i, b, p] = k[part]
                vs[i, b, p] = v[part]
        return carry

    lax.fori_loop(0, ns, proj, 0)

    def spatial_tile(step, carry):
        p = lax.rem(s + step, ns)
        for b in range(batch):
            outs = []
            for i in range(heads):
                keys = ks[i, b].reshape(ns * span, HEAD_DIM)
                vals = vs[i, b].reshape(ns * span, HEAD_DIM)
                outs.append(attend(qs[p, i, b], keys, vals, None))
            mine[0, p, b * span : (b + 1) * span, :] = jnp.concatenate(outs, axis=-1)
        pl.when(step < ns)(lambda: send_out(0, step, p).start())
        return carry

    lax.fori_loop(1, ns + 1, spatial_tile, 0)
    out_s.forward()
    out_s.finish()
    collect(0)
    fresh = project(0)
    new_s[...] = fresh
    h = add_gated(block_out[...], mod_row(mod, 1, 0, 2), fresh)
    block_out[...] = add_gated(h, mod_row(mod, 1, 1, 2), new_t[...])
    for a in range(2):
        for k in range(1, ns):
            send_out(a, k, lax.rem(s + k, ns)).wait_send()
    for c in started:
        c.wait_send()
    for part in [first, second, out_t, out_s, tokens, tokens2]:
        part.drain()


def shards(nt, ns, latent, spatial_cache, modulation, weights):
    batch, _, span, _ = latent.shape
    rows = batch * span
    block = rows // nt
    depth = weights.shape[1]
    heads = HEADS // ns
    dma = pltpu.SemaphoreType.DMA
    chunks, out_chunks = 8, 2

    def vmem(*shape):
        return VMEM(shape, jnp.bfloat16)

    args = (latent.reshape(rows, D), spatial_cache.reshape(rows, D), modulation.reshape(12, D), weights)
    outs = pl.pallas_call(
        functools.partial(kernel, nt, ns, batch),
        out_shape=[jax.ShapeDtypeStruct((rows, D), jnp.bfloat16)] * 3,
        in_specs=[pl.BlockSpec(memory_space=VMEM)] * len(args),
        out_specs=[pl.BlockSpec(memory_space=VMEM)] * 3,
        scratch_shapes=[
            vmem(ns, nt, block, D),
            vmem(ns, chunks, rows // chunks, D),
            vmem(nt, block, D),
            vmem(2, nt, depth, 4 * D // ns),
            vmem(2, ns, out_chunks, D // out_chunks, D // ns),
            vmem(2, ns, rows, D // ns),
            vmem(2, ns, rows, D // ns),
            vmem(nt, block, D),
            vmem(nt, block, D),
            vmem(ns, heads, batch, span, HEAD_DIM),
            vmem(heads, batch, ns, span, HEAD_DIM),
            vmem(heads, batch, ns, span, HEAD_DIM),
            dma((2, 3, nt)),
            dma((2, nt)),
            dma((2, ns, out_chunks)),
            dma((2, ns, out_chunks)),
            dma((nt,)),
            dma((ns, nt)),
            dma((ns, nt)),
            dma((ns, chunks)),
            dma((ns, chunks)),
            dma((2, ns)),
            dma((2, ns)),
            dma((nt,)),
            dma((nt,)),
        ],
        cost_estimate=pl.CostEstimate(flops=6_000_000_000, bytes_accessed=20_000_000, transcendentals=4_000_000),
        compiler_params=pltpu.CompilerParams(
            collective_id=0, has_side_effects=True, vmem_limit_bytes=LIMIT
        ),
    )(*args)
    return tuple(a.reshape(latent.shape) for a in outs)


def solution(mesh):
    part = P(None, "tm", "space", None)
    return jax.shard_map(
        functools.partial(shards, mesh.shape["tm"], mesh.shape["space"]),
        mesh=mesh,
        in_specs=(part, part, P(), P(None, "tm", None)),
        out_specs=(part, part, part),
        check_vma=False,
    )
```

```python
import functools

import jax
import jax.numpy as jnp
from jax import lax
from jax.experimental import pallas as pl
from jax.experimental.pallas import tpu as pltpu
from jax.sharding import PartitionSpec as P

D = 1152
HEADS = 16
HEAD_DIM = 72
MESH = pl.DeviceIdType.MESH
VMEM = pltpu.VMEM
LIMIT = 56 * 1024 * 1024


def add_gated(h, gate, branch):
    return (h.astype(jnp.float32) + gate * branch.astype(jnp.float32)).astype(jnp.bfloat16)


def modulate(h, shift, scale):
    x = h.astype(jnp.float32)
    mean = jnp.mean(x, axis=-1, keepdims=True)
    c = x - mean
    var = jnp.mean(c * c, axis=-1, keepdims=True)
    return (c * lax.rsqrt(var + 1e-06) * (1.0 + scale) + shift).astype(jnp.bfloat16)


def mod_row(mod_ref, step, attn, which):
    row = (step * 2 + attn) * 3 + which
    return mod_ref[row : row + 1, :]


def place():
    return lax.axis_index("tm"), lax.axis_index("space")


def device(t, s):
    return {"tm": t, "space": s}


def greet(peers):
    barrier = pltpu.get_barrier_semaphore()
    for t, s in peers:
        pl.semaphore_signal(barrier, inc=1, device_id=device(t, s), device_id_type=MESH)
    pl.semaphore_wait(barrier, len(peers))


def tm_peers(nt, t, s):
    return [(lax.rem(t + k, nt), s) for k in range(1, nt)]


def space_peers(ns, t, s):
    return [(t, lax.rem(s + k, ns)) for k in range(1, ns)]


def chip_peers(ns, s):
    return [lax.rem(s + 2 * k, ns) for k in range(1, ns // 2)], s + 1 - 2 * lax.rem(s, 2)


def remote(src, dst, send, recv, t, s):
    return pltpu.make_async_remote_copy(
        src_ref=src, dst_ref=dst, send_sem=send, recv_sem=recv, device_id=device(t, s), device_id_type=MESH
    )


class Spread:
    def __init__(self, slots, send, recv, ns, t, s, chunks):
        self.slots, self.send, self.recv, self.t, self.s, self.chunks = slots, send, recv, t, s, chunks
        self.others, self.sib = chip_peers(ns, s)
        self.started = []

    def copy(self, base, i, lane, n, to):
        ref = self.slots.at[base, i]
        return remote(ref, ref, self.send.at[lane, n], self.recv.at[base, i], self.t, to)

    def push(self, base, i, lane, n, to):
        c = self.copy(base, i, lane, n, to)
        c.start()
        self.started.append(c)

    def begin(self, ready=None, first=0, last=None):
        for n, i in list(enumerate(self.chunks))[first:last]:
            if ready is not None:
                ready(i)
            for k, o in enumerate(self.others):
                self.push(self.s, i, k, n, o)
            self.push(self.s, i, len(self.others), n, self.sib)

    def forward(self):
        for n, i in enumerate(self.chunks):
            for k, o in enumerate(self.others):
                self.copy(o, i, 0, 0, self.sib).wait_recv()
                self.push(o, i, len(self.others) + 1 + k, n, self.sib)

    def finish(self):
        for i in self.chunks:
            for base in [self.sib] + [o + self.sib - self.s for o in self.others]:
                self.copy(base, i, 0, 0, self.sib).wait_recv()

    def drain(self):
        for c in self.started:
            c.wait_send()


class Gather:
    def __init__(self, slots, send, recv, nt, t, s):
        self.slots, self.send, self.recv, self.s, self.t = slots, send, recv, s, t
        self.line = nt // 2
        self.z = t // 2
        self.pair = t + 1 - 2 * lax.rem(t, 2)
        self.stage_at = 0

    def copy(self, slot, kind, to):
        ref = self.slots.at[slot]
        return remote(ref, ref, self.send.at[kind, slot], self.recv.at[slot], to, self.s)

    def each(self, d, act, arrive):
        t, z, line = self.t, self.z, self.line

        def up(slot):
            pl.when(z + 1 < line)(lambda: act(self.copy(slot, 0, t + 2)))

        def down(slot):
            pl.when(z > 0)(lambda: act(self.copy(slot, 1, t - 2)))

        if d == 0:
            up(t)
            down(t)
            act(self.copy(t, 2, self.pair))
            return

        def from_below():
            slot = t - 2 * d
            if arrive:
                self.copy(slot, 2, self.pair).wait_recv()
            up(slot)
            act(self.copy(slot, 2, self.pair))

        def from_above():
            slot = t + 2 * d
            if arrive:
                self.copy(slot, 2, self.pair).wait_recv()
            down(slot)
            act(self.copy(slot, 2, self.pair))

        pl.when(z >= d)(from_below)
        pl.when(z + d < line)(from_above)

    def stage(self):
        if self.stage_at < self.line:
            self.each(self.stage_at, lambda c: c.start(), True)
            self.stage_at += 1

    def finish(self):
        while self.stage_at < self.line:
            self.stage()
        for z in range(self.line):
            self.copy(2 * z + 1 - lax.rem(self.t, 2), 2, self.pair).wait_recv()

    def drain(self):
        for d in range(self.line):
            self.each(d, lambda c: c.wait_send(), False)


def heads_of(qkv, heads):
    out = []
    for i in range(heads):
        parts = [qkv[:, (3 * i + j) * HEAD_DIM : (3 * i + j + 1) * HEAD_DIM] for j in range(3)]
        for j in range(2):
            sq = jnp.sum(parts[j] * parts[j], axis=-1, keepdims=True)
            parts[j] = parts[j] * lax.rsqrt(sq * (1.0 / HEAD_DIM) + 1e-06)
        out.append([p.astype(jnp.bfloat16) for p in parts])
    return out


def attend(q, k, v, mask):
    scores = lax.dot_general(q, k, (((1,), (1,)), ((), ())), preferred_element_type=jnp.float32)
    expo = jnp.exp(scores * (HEAD_DIM**-0.5))
    if mask is not None:
        expo = jnp.where(mask, expo, 0.0)
    probs = (expo / jnp.sum(expo, axis=-1, keepdims=True)).astype(jnp.bfloat16)
    return jnp.dot(probs, v, preferred_element_type=jnp.float32).astype(jnp.bfloat16)


def kernel(
    nt, ns, batch, lat, cache, mod, weights, block_out, new_s, new_t,
    x, x2, own, w, v, wo, mine, o, y, back, qs, ks, vs,
    send_w, recv_w, send_v, recv_v, send_wo, recv_wo, send_a, send_x, recv_x, send_x2, recv_x2, send_o, recv_o, send_y, recv_y,
):
    t, s = place()
    heads = HEADS // ns
    rows = x.shape[1] * x.shape[2]
    block = rows // nt
    span = rows // batch
    out_cols, in_cols = D // ns, 3 * D // ns
    depth = weights.shape[1]

    for i in range(ns):

        @pl.when(s == i)
        def _():
            for a in range(2):
                v[a, t] = weights[a, :, 3 * D + i * out_cols : 3 * D + (i + 1) * out_cols]
                w[a, t] = weights[a, :, i * in_cols : (i + 1) * in_cols]

    greet(tm_peers(nt, t, s) + space_peers(ns, t, s))
    qkv_s, qkv_t = [Gather(w.at[a], send_w.at[a], recv_w.at[a], nt, t, s) for a in range(2)]
    cols_s, cols_t = [Gather(v.at[a], send_v.at[a], recv_v.at[a], nt, t, s) for a in range(2)]
    qkv_t.stage()

    def fold(part, axis_in, axis_out):
        return jnp.concatenate(jnp.split(part, ns, axis=axis_in), axis=axis_out)

    def spread_out(a):
        wo[a, s] = fold(v[a].reshape(D, out_cols), 0, 1).reshape(wo.shape[2:])
        return Spread(wo.at[a], send_wo.at[a], recv_wo.at[a], ns, t, s, list(range(wo.shape[2])))

    h = add_gated(lat[...], mod_row(mod, 0, 0, 2), cache[...])
    block_out[...] = h
    own[...] = modulate(h, mod_row(mod, 0, 1, 0), mod_row(mod, 0, 1, 1)).reshape(own.shape)
    started = []
    for k in range(1, nt):
        p = lax.rem(t + k, nt)
        c = remote(own.at[p], x.at[s, t], send_a.at[k], recv_x.at[s, t], p, s)
        c.start()
        started.append(c)
    x[s, t] = own[t]
    qkv_t.stage()

    def ready(q):
        if q is not t:
            remote(own.at[0], x.at[s, q], send_a.at[0], recv_x.at[s, q], t, s).wait_recv()

    tokens = Spread(x, send_x, recv_x, ns, t, s, [t] + [lax.rem(t + nt - k, nt) for k in range(1, nt)])
    tokens.begin(ready, 0, nt // 2)
    qkv_t.stage()
    tokens.begin(ready, nt // 2, nt)
    qkv_t.stage()
    cols_t.stage()
    tokens.forward()
    qkv_t.finish()
    tokens.finish()

    mask = lax.rem(lax.broadcasted_iota(jnp.int32, (rows, rows), 0), block) == lax.rem(
        lax.broadcasted_iota(jnp.int32, (rows, rows), 1), block
    )

    def projected(a, tokens_in):
        qkv = jnp.dot(tokens_in, w[a].reshape(nt * depth, in_cols), preferred_element_type=jnp.float32)
        return heads_of(qkv, heads)

    def send_out(a, step, p):
        return remote(mine.at[a, p], o.at[a, s], send_o.at[a, step], recv_o.at[a, s], t, p)

    def temporal_tile(step, carry):
        p = lax.rem(s + step, ns)
        outs = [attend(q, k, v, mask) for q, k, v in projected(1, x[p].reshape(rows, D))]
        mine[1, p] = fold(jnp.concatenate(outs, axis=-1), 0, 1)
        pl.when(step < ns)(lambda: send_out(1, step, p).start())
        pl.when(step == 1)(cols_t.stage)
        pl.when(step == 2)(cols_t.stage)
        pl.when(step == 3)(lambda: (cols_t.stage(), cols_s.stage()) and None)
        return carry

    def collect(a):
        o[a, s] = mine[a, s]
        for k in range(1, ns):
            q = lax.rem(s + k, ns)
            remote(mine.at[a, q], o.at[a, q], send_o.at[a, k], recv_o.at[a, q], t, q).wait_recv()

    def project(a):
        attn = jnp.concatenate([fold(o[a, i], 1, 0) for i in range(ns)], axis=-1)
        cols = []
        for i in range(ns):
            weight = fold(wo[a, i].reshape(out_cols, D), 1, 0)
            cols.append(jnp.dot(attn, weight, preferred_element_type=jnp.float32).astype(jnp.bfloat16))
        return jnp.concatenate(cols, axis=-1)

    lax.fori_loop(1, ns + 1, temporal_tile, 0)
    cols_t.finish()
    out_t = spread_out(1)
    out_t.begin()
    cols_s.stage()
    qkv_s.stage()
    collect(1)
    cols_s.stage()
    out_t.forward()
    cols_s.stage()
    qkv_s.stage()
    out_t.finish()
    y[...] = project(1).reshape(y.shape)
    for k in range(1, nt):
        p = lax.rem(t + k, nt)
        c = remote(y.at[p], back.at[t], send_y.at[k], recv_y.at[t], p, s)
        c.start()
        started.append(c)
    back[t] = y[t]
    cols_s.finish()
    out_s = spread_out(0)
    out_s.begin()
    qkv_s.stage()
    for k in range(1, nt):
        q = lax.rem(t + k, nt)
        remote(y.at[q], back.at[q], send_y.at[k], recv_y.at[q], q, s).wait_recv()
    fresh = back[...].reshape(rows, D)
    new_t[...] = fresh
    h = add_gated(block_out[...], mod_row(mod, 0, 1, 2), fresh)
    block_out[...] = h
    x2[s] = modulate(h, mod_row(mod, 1, 0, 0), mod_row(mod, 1, 0, 1)).reshape(x2.shape[1:])
    tokens2 = Spread(x2, send_x2, recv_x2, ns, t, s, list(range(x2.shape[1])))
    tokens2.begin()
    qkv_s.stage()
    out_s.forward()
    tokens2.forward()
    qkv_s.finish()

    def proj(p, carry):
        p = lax.rem(s + p, ns)
        for i, (q, k, v) in enumerate(projected(0, x2[p].reshape(rows, D))):
            for b in range(batch):
                part = slice(b * span, (b + 1) * span)
                qs[p, i, b] = q[part]
                ks[i, b, p] = k[part]
                vs[i, b, p] = v[part]
        return carry

    proj(0, 0)
    tokens2.finish()
    lax.fori_loop(1, ns, proj, 0)

    def spatial_tile(step, carry):
        p = lax.rem(s + step, ns)
        parts = []
        for b in range(batch):
            outs = []
            for i in range(heads):
                keys = ks[i, b].reshape(ns * span, HEAD_DIM)
                vals = vs[i, b].reshape(ns * span, HEAD_DIM)
                outs.append(attend(qs[p, i, b], keys, vals, None))
            parts.append(jnp.concatenate(outs, axis=-1))
        mine[0, p] = fold(jnp.concatenate(parts, axis=0), 0, 1)
        pl.when(step < ns)(lambda: send_out(0, step, p).start())
        return carry

    lax.fori_loop(1, ns + 1, spatial_tile, 0)
    out_s.finish()
    collect(0)
    fresh = project(0)
    new_s[...] = fresh
    h = add_gated(block_out[...], mod_row(mod, 1, 0, 2), fresh)
    block_out[...] = add_gated(h, mod_row(mod, 1, 1, 2), new_t[...])
    for a in range(2):
        for k in range(1, ns):
            send_out(a, k, lax.rem(s + k, ns)).wait_send()
    for c in started:
        c.wait_send()
    for part in [qkv_t, cols_t, qkv_s, cols_s, out_t, out_s, tokens, tokens2]:
        part.drain()


def shards(nt, ns, latent, spatial_cache, modulation, weights):
    batch, _, span, _ = latent.shape
    rows = batch * span
    block = rows // nt
    depth = weights.shape[1]
    heads = HEADS // ns
    dma = pltpu.SemaphoreType.DMA
    chunks, out_chunks = 8, 2 if D // ns % 32 == 0 else 1

    def vmem(*shape):
        return VMEM(shape, jnp.bfloat16)

    args = (latent.reshape(rows, D), spatial_cache.reshape(rows, D), modulation.reshape(12, D), weights)
    outs = pl.pallas_call(
        functools.partial(kernel, nt, ns, batch),
        out_shape=[jax.ShapeDtypeStruct((rows, D), jnp.bfloat16)] * 3,
        in_specs=[pl.BlockSpec(memory_space=VMEM)] * len(args),
        out_specs=[pl.BlockSpec(memory_space=VMEM)] * 3,
        scratch_shapes=[
            vmem(ns, nt, block, D),
            vmem(ns, chunks, rows // chunks, D),
            vmem(nt, block, D),
            vmem(2, nt, depth, 3 * D // ns),
            vmem(2, nt, depth, D // ns),
            vmem(2, ns, out_chunks, D // ns // out_chunks, D),
            vmem(2, ns, rows // ns, D),
            vmem(2, ns, rows // ns, D),
            vmem(nt, block, D),
            vmem(nt, block, D),
            vmem(ns, heads, batch, span, HEAD_DIM),
            vmem(heads, batch, ns, span, HEAD_DIM),
            vmem(heads, batch, ns, span, HEAD_DIM),
            dma((2, 3, nt)),
            dma((2, nt)),
            dma((2, 3, nt)),
            dma((2, nt)),
            dma((2, ns, out_chunks)),
            dma((2, ns, out_chunks)),
            dma((nt,)),
            dma((ns, nt)),
            dma((ns, nt)),
            dma((ns, chunks)),
            dma((ns, chunks)),
            dma((2, ns)),
            dma((2, ns)),
            dma((nt,)),
            dma((nt,)),
        ],
        cost_estimate=pl.CostEstimate(flops=6_000_000_000, bytes_accessed=20_000_000, transcendentals=4_000_000),
        compiler_params=pltpu.CompilerParams(
            collective_id=0, has_side_effects=True, vmem_limit_bytes=LIMIT
        ),
    )(*args)
    return tuple(a.reshape(latent.shape) for a in outs)


def solution(mesh):
    part = P(None, "tm", "space", None)
    return jax.shard_map(
        functools.partial(shards, mesh.shape["tm"], mesh.shape["space"]),
        mesh=mesh,
        in_specs=(part, part, P(), P(None, "tm", None)),
        out_specs=(part, part, part),
        check_vma=False,
    )
```

```python
import functools

import jax
import jax.numpy as jnp
from jax import lax
from jax.experimental import pallas as pl
from jax.experimental.pallas import tpu as pltpu
from jax.sharding import PartitionSpec as P

D = 1152
HEADS = 16
HEAD_DIM = 72
LANES = 128
LOG2E = 1.4426950408889634
QUERIES = 512
MESH = pl.DeviceIdType.MESH
VMEM = pltpu.VMEM
LIMIT = 56 * 1024 * 1024


def add_gated(h, gate, branch):
    return (h.astype(jnp.float32) + gate * branch.astype(jnp.float32)).astype(jnp.bfloat16)


def modulate(h, shift, scale):
    x = h.astype(jnp.float32)
    mean = jnp.mean(x, axis=-1, keepdims=True)
    c = x - mean
    var = jnp.mean(c * c, axis=-1, keepdims=True)
    return (c * lax.rsqrt(var + 1e-06) * (1.0 + scale) + shift).astype(jnp.bfloat16)


def mod_row(mod_ref, step, attn, which):
    row = (step * 2 + attn) * 3 + which
    return mod_ref[row : row + 1, :]


def place():
    return lax.axis_index("tm"), lax.axis_index("space")


def device(t, s):
    return {"tm": t, "space": s}


def greet(peers):
    barrier = pltpu.get_barrier_semaphore()
    for t, s in peers:
        pl.semaphore_signal(barrier, inc=1, device_id=device(t, s), device_id_type=MESH)
    pl.semaphore_wait(barrier, len(peers))


def tm_peers(nt, t, s):
    return [(lax.rem(t + k, nt), s) for k in range(1, nt)]


def space_peers(ns, t, s):
    return [(t, lax.rem(s + k, ns)) for k in range(1, ns)]


def chip_peers(ns, s):
    return [lax.rem(s + 2 * k, ns) for k in range(1, ns // 2)], s + 1 - 2 * lax.rem(s, 2)


def remote(src, dst, send, recv, t, s):
    return pltpu.make_async_remote_copy(
        src_ref=src, dst_ref=dst, send_sem=send, recv_sem=recv, device_id=device(t, s), device_id_type=MESH
    )


class Spread:
    def __init__(self, slots, send, recv, ns, t, s, chunks):
        self.slots, self.send, self.recv, self.t, self.s, self.chunks = slots, send, recv, t, s, chunks
        self.others, self.sib = chip_peers(ns, s)
        self.started = []

    def copy(self, base, i, lane, n, to):
        ref = self.slots.at[base, i]
        return remote(ref, ref, self.send.at[lane, n], self.recv.at[base, i], self.t, to)

    def push(self, base, i, lane, n, to):
        c = self.copy(base, i, lane, n, to)
        c.start()
        self.started.append(c)

    def begin(self, ready=None, first=0, last=None):
        for n, i in list(enumerate(self.chunks))[first:last]:
            if ready is not None:
                ready(i)
            for k, o in enumerate(self.others):
                self.push(self.s, i, k, n, o)
            self.push(self.s, i, len(self.others), n, self.sib)

    def forward(self):
        for n, i in enumerate(self.chunks):
            for k, o in enumerate(self.others):
                self.copy(o, i, 0, 0, self.sib).wait_recv()
                self.push(o, i, len(self.others) + 1 + k, n, self.sib)

    def finish(self):
        for i in self.chunks:
            for base in [self.sib] + [o + self.sib - self.s for o in self.others]:
                self.copy(base, i, 0, 0, self.sib).wait_recv()

    def drain(self):
        for c in self.started:
            c.wait_send()


class Gather:
    def __init__(self, slots, send, recv, nt, t, s):
        self.slots, self.send, self.recv, self.s, self.t = slots, send, recv, s, t
        self.line = nt // 2
        self.z = t // 2
        self.pair = t + 1 - 2 * lax.rem(t, 2)
        self.stage_at = 0

    def copy(self, slot, kind, to):
        ref = self.slots.at[slot]
        return remote(ref, ref, self.send.at[kind, slot], self.recv.at[slot], to, self.s)

    def each(self, d, act, arrive):
        t, z, line = self.t, self.z, self.line

        def up(slot):
            pl.when(z + 1 < line)(lambda: act(self.copy(slot, 0, t + 2)))

        def down(slot):
            pl.when(z > 0)(lambda: act(self.copy(slot, 1, t - 2)))

        if d == 0:
            up(t)
            down(t)
            act(self.copy(t, 2, self.pair))
            return

        def from_below():
            slot = t - 2 * d
            if arrive:
                self.copy(slot, 2, self.pair).wait_recv()
            up(slot)
            act(self.copy(slot, 2, self.pair))

        def from_above():
            slot = t + 2 * d
            if arrive:
                self.copy(slot, 2, self.pair).wait_recv()
            down(slot)
            act(self.copy(slot, 2, self.pair))

        pl.when(z >= d)(from_below)
        pl.when(z + d < line)(from_above)

    def stage(self):
        if self.stage_at < self.line:
            self.each(self.stage_at, lambda c: c.start(), True)
            self.stage_at += 1

    def finish(self):
        while self.stage_at < self.line:
            self.stage()
        for z in range(self.line):
            self.copy(2 * z + 1 - lax.rem(self.t, 2), 2, self.pair).wait_recv()

    def drain(self):
        for d in range(self.line):
            self.each(d, lambda c: c.wait_send(), False)


def heads_of(qkv, heads):
    out = []
    for i in range(heads):
        parts = [qkv[:, (3 * i + j) * HEAD_DIM : (3 * i + j + 1) * HEAD_DIM] for j in range(3)]
        for j in range(2):
            sq = jnp.sum(parts[j] * parts[j], axis=-1, keepdims=True)
            parts[j] = parts[j] * lax.rsqrt(sq * (1.0 / HEAD_DIM) + 1e-06)
        out.append([p.astype(jnp.bfloat16) for p in parts])
    return out


def attend(q, k, v, mask):
    scores = lax.dot_general(q, k, (((1,), (1,)), ((), ())), preferred_element_type=jnp.float32)
    expo = jnp.exp2(scores * (HEAD_DIM**-0.5 * LOG2E)).astype(jnp.bfloat16)
    if mask is not None:
        expo = expo * mask
    out = jnp.dot(expo, v, preferred_element_type=jnp.float32)
    return (out[:, :HEAD_DIM] * (1.0 / out[:, HEAD_DIM : HEAD_DIM + 1])).astype(jnp.bfloat16)


def with_ones(v):
    return jnp.concatenate([v, jnp.ones((v.shape[0], LANES - HEAD_DIM), v.dtype)], axis=-1)


def kernel(
    nt, ns, batch, lat, cache, mod, weights, block_out, new_s, new_t,
    x, x2, own, w, v, wo, mine, o, mine_s, o_s, y, back, qs, ks, vs,
    send_w, recv_w, send_v, recv_v, send_wo, recv_wo, send_a, send_x, recv_x, send_x2, recv_x2, send_o, recv_o, send_s, recv_s, send_y, recv_y,
):
    t, s = place()
    heads = HEADS // ns
    rows = x.shape[1] * x.shape[2]
    block = rows // nt
    span = rows // batch
    out_cols, in_cols = D // ns, 3 * D // ns
    depth = weights.shape[1]

    for i in range(ns):

        @pl.when(s == i)
        def _():
            for a in range(2):
                v[a, t] = weights[a, :, 3 * D + i * out_cols : 3 * D + (i + 1) * out_cols]
                w[a, t] = weights[a, :, i * in_cols : (i + 1) * in_cols]

    greet(tm_peers(nt, t, s) + space_peers(ns, t, s))
    qkv_s, qkv_t = [Gather(w.at[a], send_w.at[a], recv_w.at[a], nt, t, s) for a in range(2)]
    cols_s, cols_t = [Gather(v.at[a], send_v.at[a], recv_v.at[a], nt, t, s) for a in range(2)]
    qkv_t.stage()

    def fold(part, axis_in, axis_out):
        return jnp.concatenate(jnp.split(part, ns, axis=axis_in), axis=axis_out)

    def spread_out(a):
        wo[a, s] = fold(v[a].reshape(D, out_cols), 0, 1).reshape(wo.shape[2:])
        return Spread(wo.at[a], send_wo.at[a], recv_wo.at[a], ns, t, s, list(range(wo.shape[2])))

    h = add_gated(lat[...], mod_row(mod, 0, 0, 2), cache[...])
    block_out[...] = h
    own[...] = modulate(h, mod_row(mod, 0, 1, 0), mod_row(mod, 0, 1, 1)).reshape(own.shape)
    started = []
    for k in range(1, nt):
        p = lax.rem(t + k, nt)
        c = remote(own.at[p], x.at[s, t], send_a.at[k], recv_x.at[s, t], p, s)
        c.start()
        started.append(c)
    x[s, t] = own[t]
    qkv_t.stage()

    def ready(q):
        if q is not t:
            remote(own.at[0], x.at[s, q], send_a.at[0], recv_x.at[s, q], t, s).wait_recv()

    tokens = Spread(x, send_x, recv_x, ns, t, s, [t] + [lax.rem(t + nt - k, nt) for k in range(1, nt)])
    tokens.begin(ready, 0, nt // 2)
    qkv_t.stage()
    tokens.begin(ready, nt // 2, nt)
    qkv_t.stage()
    cols_t.stage()
    tokens.forward()
    qkv_t.finish()
    tokens.finish()

    mask = lax.rem(lax.broadcasted_iota(jnp.int32, (rows, rows), 0), block) == lax.rem(
        lax.broadcasted_iota(jnp.int32, (rows, rows), 1), block
    )
    mask = jnp.where(mask, 1.0, 0.0).astype(jnp.bfloat16)

    def projected(a, tokens_in):
        qkv = jnp.dot(tokens_in, w[a].reshape(nt * depth, in_cols), preferred_element_type=jnp.float32)
        return heads_of(qkv, heads)

    def send_out(step, p):
        return remote(mine.at[p], o.at[s], send_o.at[step], recv_o.at[s], t, p)

    def send_batch(b, k):
        q = lax.rem(s + k, ns)
        return remote(mine_s.at[b, q], o_s.at[b, s], send_s.at[b, k], recv_s.at[b, s], t, q)

    groups = span // mine_s.shape[2]

    def fold_rows(part):
        return jnp.concatenate(jnp.split(part, groups, axis=0), axis=1)

    def unfold_rows(part):
        return jnp.concatenate(jnp.split(part, groups, axis=1), axis=0)

    def temporal_tile(step, carry):
        p = lax.rem(s + step, ns)
        outs = [attend(q, k, with_ones(v), mask) for q, k, v in projected(1, x[p].reshape(rows, D))]
        mine[p] = fold(jnp.concatenate(outs, axis=-1), 0, 1)
        pl.when(step < ns)(lambda: send_out(step, p).start())
        pl.when(step == 1)(cols_t.stage)
        pl.when(step == 2)(cols_t.stage)
        pl.when(step == 3)(lambda: (cols_t.stage(), cols_s.stage()) and None)
        return carry

    def collect():
        o[s] = mine[s]
        for k in range(1, ns):
            q = lax.rem(s + k, ns)
            remote(mine.at[q], o.at[q], send_o.at[k], recv_o.at[q], t, q).wait_recv()

    def project(a, parts):
        attn = jnp.concatenate(parts, axis=-1)
        cols = []
        for i in range(ns):
            weight = fold(wo[a, i].reshape(out_cols, D), 1, 0)
            cols.append(jnp.dot(attn, weight, preferred_element_type=jnp.float32).astype(jnp.bfloat16))
        return jnp.concatenate(cols, axis=-1)

    lax.fori_loop(1, ns + 1, temporal_tile, 0)
    cols_t.finish()
    out_t = spread_out(1)
    out_t.begin()
    cols_s.stage()
    qkv_s.stage()
    collect()
    cols_s.stage()
    out_t.forward()
    cols_s.stage()
    qkv_s.stage()
    out_t.finish()
    y[...] = project(1, [fold(o[i], 1, 0) for i in range(ns)]).reshape(y.shape)
    for k in range(1, nt):
        p = lax.rem(t + k, nt)
        c = remote(y.at[p], back.at[t], send_y.at[k], recv_y.at[t], p, s)
        c.start()
        started.append(c)
    back[t] = y[t]
    cols_s.finish()
    out_s = spread_out(0)
    out_s.begin()
    qkv_s.stage()

    def returned(q):
        if q is not t:
            remote(y.at[q], back.at[q], send_y.at[0], recv_y.at[q], t, s).wait_recv()
        at = pl.ds(pl.multiple_of(q * block, block), block)
        new_t[at, :] = back[q]
        h = add_gated(block_out[at, :], mod_row(mod, 0, 1, 2), back[q])
        block_out[at, :] = h
        x2[s, q] = modulate(h, mod_row(mod, 1, 0, 0), mod_row(mod, 1, 0, 1))

    tokens2 = Spread(x2, send_x2, recv_x2, ns, t, s, [t] + [lax.rem(t + nt - k, nt) for k in range(1, nt)])
    tokens2.begin(returned)
    qkv_s.stage()
    out_s.forward()
    tokens2.forward()
    qkv_s.finish()

    def proj(p, carry):
        p = lax.rem(s + p, ns)
        for i, (q, k, v) in enumerate(projected(0, x2[p].reshape(rows, D))):
            for b in range(batch):
                part = slice(b * span, (b + 1) * span)
                qs[i, b, p] = q[part]
                ks[i, b, p] = k[part]
                vs[i, b, p] = with_ones(v[part])
        return carry

    proj(0, 0)
    tokens2.finish()
    lax.fori_loop(1, ns, proj, 0)

    def spatial_batch(b, carry):
        total = ns * span
        step = min(QUERIES, total)
        parts = [[] for _ in range(total // step)]
        for i in range(heads):
            queries = qs[i, b].reshape(total, HEAD_DIM)
            keys = ks[i, b].reshape(total, HEAD_DIM)
            vals = vs[i, b].reshape(total, LANES)
            for j, part in enumerate(parts):
                part.append(attend(queries[j * step : (j + 1) * step], keys, vals, None))
        attn = jnp.concatenate([jnp.concatenate(part, axis=-1) for part in parts], axis=0)
        for i in range(ns):
            mine_s[b, i] = fold_rows(attn[i * span : (i + 1) * span])
        for k in range(1, ns):
            send_batch(b, k).start()
        return carry

    lax.fori_loop(0, batch, spatial_batch, 0)
    for b in range(batch):
        o_s[b, s] = mine_s[b, s]
        for k in range(1, ns):
            q = lax.rem(s + k, ns)
            remote(mine_s.at[b, q], o_s.at[b, q], send_s.at[b, k], recv_s.at[b, q], t, q).wait_recv()
    out_s.finish()
    fresh = project(0, [jnp.concatenate([unfold_rows(o_s[b, i]) for b in range(batch)], axis=0) for i in range(ns)])
    new_s[...] = fresh
    h = add_gated(block_out[...], mod_row(mod, 1, 0, 2), fresh)
    block_out[...] = add_gated(h, mod_row(mod, 1, 1, 2), new_t[...])
    for k in range(1, ns):
        send_out(k, lax.rem(s + k, ns)).wait_send()
        for b in range(batch):
            send_batch(b, k).wait_send()
    for c in started:
        c.wait_send()
    for part in [qkv_t, cols_t, qkv_s, cols_s, out_t, out_s, tokens, tokens2]:
        part.drain()


def shards(nt, ns, latent, spatial_cache, modulation, weights):
    batch, _, span, _ = latent.shape
    rows = batch * span
    block = rows // nt
    depth = weights.shape[1]
    heads = HEADS // ns
    dma = pltpu.SemaphoreType.DMA
    out_chunks = 2 if D // ns % 32 == 0 else 1
    groups = min(ns, span // 16)

    def vmem(*shape):
        return VMEM(shape, jnp.bfloat16)

    args = (latent.reshape(rows, D), spatial_cache.reshape(rows, D), modulation.reshape(12, D), weights)
    outs = pl.pallas_call(
        functools.partial(kernel, nt, ns, batch),
        out_shape=[jax.ShapeDtypeStruct((rows, D), jnp.bfloat16)] * 3,
        in_specs=[pl.BlockSpec(memory_space=VMEM)] * len(args),
        out_specs=[pl.BlockSpec(memory_space=VMEM)] * 3,
        scratch_shapes=[
            vmem(ns, nt, block, D),
            vmem(ns, nt, block, D),
            vmem(nt, block, D),
            vmem(2, nt, depth, 3 * D // ns),
            vmem(2, nt, depth, D // ns),
            vmem(2, ns, out_chunks, D // ns // out_chunks, D),
            vmem(ns, rows // ns, D),
            vmem(ns, rows // ns, D),
            vmem(batch, ns, span // groups, D // ns * groups),
            vmem(batch, ns, span // groups, D // ns * groups),
            vmem(nt, block, D),
            vmem(nt, block, D),
            vmem(heads, batch, ns, span, HEAD_DIM),
            vmem(heads, batch, ns, span, HEAD_DIM),
            vmem(heads, batch, ns, span, LANES),
            dma((2, 3, nt)),
            dma((2, nt)),
            dma((2, 3, nt)),
            dma((2, nt)),
            dma((2, ns, out_chunks)),
            dma((2, ns, out_chunks)),
            dma((nt,)),
            dma((ns, nt)),
            dma((ns, nt)),
            dma((ns, nt)),
            dma((ns, nt)),
            dma((ns,)),
            dma((ns,)),
            dma((batch, ns)),
            dma((batch, ns)),
            dma((nt,)),
            dma((nt,)),
        ],
        cost_estimate=pl.CostEstimate(flops=6_000_000_000, bytes_accessed=20_000_000, transcendentals=4_000_000),
        compiler_params=pltpu.CompilerParams(
            collective_id=0, has_side_effects=True, vmem_limit_bytes=LIMIT
        ),
    )(*args)
    return tuple(a.reshape(latent.shape) for a in outs)


def solution(mesh):
    part = P(None, "tm", "space", None)
    return jax.shard_map(
        functools.partial(shards, mesh.shape["tm"], mesh.shape["space"]),
        mesh=mesh,
        in_specs=(part, part, P(), P(None, "tm", None)),
        out_specs=(part, part, part),
        check_vma=False,
    )
```

```python
import functools

import jax
import jax.numpy as jnp
from jax import lax
from jax.experimental import pallas as pl
from jax.experimental.pallas import tpu as pltpu
from jax.sharding import PartitionSpec as P

D = 1152
HEADS = 16
HEAD_DIM = 72
LANES = 128
LOG2E = 1.4426950408889634
QUERIES = 512
MESH = pl.DeviceIdType.MESH
VMEM = pltpu.VMEM
LIMIT = 56 * 1024 * 1024


def add_gated(h, gate, branch):
    return (h.astype(jnp.float32) + gate * branch.astype(jnp.float32)).astype(jnp.bfloat16)


def modulate(h, shift, scale):
    x = h.astype(jnp.float32)
    mean = jnp.mean(x, axis=-1, keepdims=True)
    c = x - mean
    var = jnp.mean(c * c, axis=-1, keepdims=True)
    return (c * lax.rsqrt(var + 1e-06) * (1.0 + scale) + shift).astype(jnp.bfloat16)


def mod_row(mod_ref, step, attn, which):
    return mod_ref[step, attn, which : which + 1, :]


def place():
    return lax.axis_index("tm"), lax.axis_index("space")


def device(t, s):
    return {"tm": t, "space": s}


def greet(peers):
    barrier = pltpu.get_barrier_semaphore()
    for t, s in peers:
        pl.semaphore_signal(barrier, inc=1, device_id=device(t, s), device_id_type=MESH)
    pl.semaphore_wait(barrier, len(peers))


def tm_peers(nt, t, s):
    return [(lax.rem(t + k, nt), s) for k in range(1, nt)]


def space_peers(ns, t, s):
    return [(t, lax.rem(s + k, ns)) for k in range(1, ns)]


def chip_peers(ns, s):
    return [lax.rem(s + 2 * k, ns) for k in range(1, ns // 2)], s + 1 - 2 * lax.rem(s, 2)


def remote(src, dst, send, recv, t, s):
    return pltpu.make_async_remote_copy(
        src_ref=src, dst_ref=dst, send_sem=send, recv_sem=recv, device_id=device(t, s), device_id_type=MESH
    )


class Spread:
    def __init__(self, slots, send, recv, ns, t, s, chunks):
        self.slots, self.send, self.recv, self.t, self.s, self.chunks = slots, send, recv, t, s, chunks
        self.others, self.sib = chip_peers(ns, s)
        self.started = []

    def copy(self, base, i, lane, n, to):
        ref = self.slots.at[base, i]
        return remote(ref, ref, self.send.at[lane, n], self.recv.at[base, i], self.t, to)

    def push(self, base, i, lane, n, to):
        c = self.copy(base, i, lane, n, to)
        c.start()
        self.started.append(c)

    def begin(self, ready=None, first=0, last=None):
        for n, i in list(enumerate(self.chunks))[first:last]:
            if ready is not None:
                ready(i)
            for k, o in enumerate(self.others):
                self.push(self.s, i, k, n, o)
            self.push(self.s, i, len(self.others), n, self.sib)

    def forward(self):
        for n, i in enumerate(self.chunks):
            for k, o in enumerate(self.others):
                self.copy(o, i, 0, 0, self.sib).wait_recv()
                self.push(o, i, len(self.others) + 1 + k, n, self.sib)

    def finish(self):
        for i in self.chunks:
            for base in [self.sib] + [o + self.sib - self.s for o in self.others]:
                self.copy(base, i, 0, 0, self.sib).wait_recv()

    def drain(self):
        for c in self.started:
            c.wait_send()


class Gather:
    def __init__(self, slots, send, recv, nt, t, s):
        self.slots, self.send, self.recv, self.s, self.t = slots, send, recv, s, t
        self.line = nt // 2
        self.z = t // 2
        self.pair = t + 1 - 2 * lax.rem(t, 2)
        self.stage_at = 0

    def copy(self, slot, kind, to):
        ref = self.slots.at[slot]
        return remote(ref, ref, self.send.at[kind, slot], self.recv.at[slot], to, self.s)

    def each(self, d, act, arrive):
        t, z, line = self.t, self.z, self.line

        def up(slot):
            pl.when(z + 1 < line)(lambda: act(self.copy(slot, 0, t + 2)))

        def down(slot):
            pl.when(z > 0)(lambda: act(self.copy(slot, 1, t - 2)))

        if d == 0:
            up(t)
            down(t)
            act(self.copy(t, 2, self.pair))
            return

        def from_below():
            slot = t - 2 * d
            if arrive:
                self.copy(slot, 2, self.pair).wait_recv()
            up(slot)
            act(self.copy(slot, 2, self.pair))

        def from_above():
            slot = t + 2 * d
            if arrive:
                self.copy(slot, 2, self.pair).wait_recv()
            down(slot)
            act(self.copy(slot, 2, self.pair))

        pl.when(z >= d)(from_below)
        pl.when(z + d < line)(from_above)

    def stage(self):
        if self.stage_at < self.line:
            self.each(self.stage_at, lambda c: c.start(), True)
            self.stage_at += 1

    def finish(self):
        while self.stage_at < self.line:
            self.stage()
        for z in range(self.line):
            self.copy(2 * z + 1 - lax.rem(self.t, 2), 2, self.pair).wait_recv()

    def drain(self):
        for d in range(self.line):
            self.each(d, lambda c: c.wait_send(), False)


def heads_of(qkv, heads):
    out = []
    for i in range(heads):
        parts = [qkv[:, (3 * i + j) * HEAD_DIM : (3 * i + j + 1) * HEAD_DIM] for j in range(3)]
        for j in range(2):
            sq = jnp.sum(parts[j] * parts[j], axis=-1, keepdims=True)
            parts[j] = parts[j] * lax.rsqrt(sq * (1.0 / HEAD_DIM) + 1e-06)
        out.append([p.astype(jnp.bfloat16) for p in parts])
    return out


def attend(q, k, v, mask):
    scores = lax.dot_general(q, k, (((1,), (1,)), ((), ())), preferred_element_type=jnp.float32)
    expo = jnp.exp2(scores * (HEAD_DIM**-0.5 * LOG2E)).astype(jnp.bfloat16)
    if mask is not None:
        expo = expo * mask
    out = jnp.dot(expo, v, preferred_element_type=jnp.float32)
    return (out[:, :HEAD_DIM] * (1.0 / out[:, HEAD_DIM : HEAD_DIM + 1])).astype(jnp.bfloat16)


def with_ones(v):
    return jnp.concatenate([v, jnp.ones((v.shape[0], LANES - HEAD_DIM), v.dtype)], axis=-1)


def kernel(
    nt, ns, batch, lat, cache, mod, weights, block_out, new_s, new_t,
    x, x2, own, w, v, wo, mine, o, mine_s, o_s, y, back, qs, ks, vs,
    send_w, recv_w, send_v, recv_v, send_wo, recv_wo, send_a, send_x, recv_x, send_x2, recv_x2, send_o, recv_o, send_s, recv_s, send_y, recv_y,
):
    t, s = place()
    heads = HEADS // ns
    rows = x.shape[1] * x.shape[2]
    block = rows // nt
    span = rows // batch
    out_cols, in_cols = D // ns, 3 * D // ns
    depth = weights.shape[1]

    for i in range(ns):

        @pl.when(s == i)
        def _():
            for a in range(2):
                v[a, t] = weights[a, :, 3 * D + i * out_cols : 3 * D + (i + 1) * out_cols]
                w[a, t] = weights[a, :, i * in_cols : (i + 1) * in_cols]

    greet(tm_peers(nt, t, s) + space_peers(ns, t, s))
    qkv_s, qkv_t = [Gather(w.at[a], send_w.at[a], recv_w.at[a], nt, t, s) for a in range(2)]
    cols_s, cols_t = [Gather(v.at[a], send_v.at[a], recv_v.at[a], nt, t, s) for a in range(2)]
    qkv_t.stage()

    def fold(part, axis_in, axis_out):
        return jnp.concatenate(jnp.split(part, ns, axis=axis_in), axis=axis_out)

    def spread_out(a):
        wo[a, s] = fold(v[a].reshape(D, out_cols), 0, 1).reshape(wo.shape[2:])
        return Spread(wo.at[a], send_wo.at[a], recv_wo.at[a], ns, t, s, list(range(wo.shape[2])))

    h = add_gated(lat[...], mod_row(mod, 0, 0, 2), cache[...])
    block_out[...] = h
    own[...] = modulate(h, mod_row(mod, 0, 1, 0), mod_row(mod, 0, 1, 1)).reshape(own.shape)
    started = []
    for k in range(1, nt):
        p = lax.rem(t + k, nt)
        c = remote(own.at[p], x.at[s, t], send_a.at[k], recv_x.at[s, t], p, s)
        c.start()
        started.append(c)
    x[s, t] = own[t]
    qkv_t.stage()

    def ready(q):
        if q is not t:
            remote(own.at[0], x.at[s, q], send_a.at[0], recv_x.at[s, q], t, s).wait_recv()

    tokens = Spread(x, send_x, recv_x, ns, t, s, [t] + [lax.rem(t + nt - k, nt) for k in range(1, nt)])
    tokens.begin(ready, 0, nt // 2)
    qkv_t.stage()
    tokens.begin(ready, nt // 2, nt)
    qkv_t.stage()
    cols_t.stage()
    tokens.forward()
    qkv_t.finish()
    tokens.finish()

    mask = lax.rem(lax.broadcasted_iota(jnp.int32, (rows, rows), 0), block) == lax.rem(
        lax.broadcasted_iota(jnp.int32, (rows, rows), 1), block
    )
    mask = jnp.where(mask, 1.0, 0.0).astype(jnp.bfloat16)

    def projected(a, tokens_in):
        qkv = jnp.dot(tokens_in, w[a].reshape(nt * depth, in_cols), preferred_element_type=jnp.float32)
        return heads_of(qkv, heads)

    def send_out(step, p):
        return remote(mine.at[p], o.at[s], send_o.at[step], recv_o.at[s], t, p)

    def send_batch(b, k):
        q = lax.rem(s + k, ns)
        return remote(mine_s.at[b, q], o_s.at[b, s], send_s.at[b, k], recv_s.at[b, s], t, q)

    groups = span // mine_s.shape[2]

    def fold_rows(part):
        return jnp.concatenate(jnp.split(part, groups, axis=0), axis=1)

    def unfold_rows(part):
        return jnp.concatenate(jnp.split(part, groups, axis=1), axis=0)

    def temporal_tile(step, carry):
        p = lax.rem(s + step, ns)
        outs = [attend(q, k, with_ones(v), mask) for q, k, v in projected(1, x[p].reshape(rows, D))]
        mine[p] = fold(jnp.concatenate(outs, axis=-1), 0, 1)
        pl.when(step < ns)(lambda: send_out(step, p).start())
        pl.when(step == 1)(cols_t.stage)
        pl.when(step == 2)(cols_t.stage)
        pl.when(step == 3)(lambda: (cols_t.stage(), cols_s.stage()) and None)
        return carry

    def collect():
        o[s] = mine[s]
        for k in range(1, ns):
            q = lax.rem(s + k, ns)
            remote(mine.at[q], o.at[q], send_o.at[k], recv_o.at[q], t, q).wait_recv()

    def project(a, parts):
        attn = jnp.concatenate(parts, axis=-1)
        cols = []
        for i in range(ns):
            weight = fold(wo[a, i].reshape(out_cols, D), 1, 0)
            cols.append(jnp.dot(attn, weight, preferred_element_type=jnp.float32).astype(jnp.bfloat16))
        return jnp.concatenate(cols, axis=-1)

    lax.fori_loop(1, ns + 1, temporal_tile, 0)
    cols_t.finish()
    out_t = spread_out(1)
    out_t.begin()
    cols_s.stage()
    qkv_s.stage()
    collect()
    cols_s.stage()
    out_t.forward()
    cols_s.stage()
    qkv_s.stage()
    out_t.finish()
    y[...] = project(1, [fold(o[i], 1, 0) for i in range(ns)]).reshape(y.shape)
    for k in range(1, nt):
        p = lax.rem(t + k, nt)
        c = remote(y.at[p], back.at[t], send_y.at[k], recv_y.at[t], p, s)
        c.start()
        started.append(c)
    back[t] = y[t]
    cols_s.finish()
    out_s = spread_out(0)
    out_s.begin()
    qkv_s.stage()

    def returned(q):
        if q is not t:
            remote(y.at[q], back.at[q], send_y.at[0], recv_y.at[q], t, s).wait_recv()
        at = pl.ds(pl.multiple_of(q * block, block), block)
        new_t[at, :] = back[q]
        h = add_gated(block_out[at, :], mod_row(mod, 0, 1, 2), back[q])
        block_out[at, :] = h
        x2[s, q] = modulate(h, mod_row(mod, 1, 0, 0), mod_row(mod, 1, 0, 1))

    tokens2 = Spread(x2, send_x2, recv_x2, ns, t, s, [t] + [lax.rem(t + nt - k, nt) for k in range(1, nt)])
    tokens2.begin(returned)
    qkv_s.stage()
    out_s.forward()
    tokens2.forward()
    qkv_s.finish()

    def proj(p, carry):
        p = lax.rem(s + p, ns)
        for i, (q, k, v) in enumerate(projected(0, x2[p].reshape(rows, D))):
            for b in range(batch):
                part = slice(b * span, (b + 1) * span)
                qs[i, b, p] = q[part]
                ks[i, b, p] = k[part]
                vs[i, b, p] = with_ones(v[part])
        return carry

    proj(0, 0)
    tokens2.finish()
    lax.fori_loop(1, ns, proj, 0)

    def spatial_batch(b, carry):
        total = ns * span
        step = min(QUERIES, total)
        parts = [[] for _ in range(total // step)]
        for i in range(heads):
            queries = qs[i, b].reshape(total, HEAD_DIM)
            keys = ks[i, b].reshape(total, HEAD_DIM)
            vals = vs[i, b].reshape(total, LANES)
            for j, part in enumerate(parts):
                part.append(attend(queries[j * step : (j + 1) * step], keys, vals, None))
        attn = jnp.concatenate([jnp.concatenate(part, axis=-1) for part in parts], axis=0)
        for i in range(ns):
            mine_s[b, i] = fold_rows(attn[i * span : (i + 1) * span])
        for k in range(1, ns):
            send_batch(b, k).start()
        return carry

    lax.fori_loop(0, batch, spatial_batch, 0)
    for b in range(batch):
        o_s[b, s] = mine_s[b, s]
        for k in range(1, ns):
            q = lax.rem(s + k, ns)
            remote(mine_s.at[b, q], o_s.at[b, q], send_s.at[b, k], recv_s.at[b, q], t, q).wait_recv()
    out_s.finish()
    fresh = project(0, [jnp.concatenate([unfold_rows(o_s[b, i]) for b in range(batch)], axis=0) for i in range(ns)])
    new_s[...] = fresh
    h = add_gated(block_out[...], mod_row(mod, 1, 0, 2), fresh)
    block_out[...] = add_gated(h, mod_row(mod, 1, 1, 2), new_t[...])
    for k in range(1, ns):
        send_out(k, lax.rem(s + k, ns)).wait_send()
        for b in range(batch):
            send_batch(b, k).wait_send()
    for c in started:
        c.wait_send()
    for part in [qkv_t, cols_t, qkv_s, cols_s, out_t, out_s, tokens, tokens2]:
        part.drain()


def leave_kernel(*refs):
    for i in range(3):
        refs[3 + i][...] = refs[i][...]


def shards(nt, ns, latent, spatial_cache, modulation, weights):
    batch, _, span, _ = latent.shape
    rows = batch * span
    block = rows // nt
    depth = weights.shape[1]
    heads = HEADS // ns
    dma = pltpu.SemaphoreType.DMA
    out_chunks = 2 if D // ns % 32 == 0 else 1
    groups = min(ns, span // 16)

    def vmem(*shape):
        return VMEM(shape, jnp.bfloat16)

    args = (latent.reshape(rows, D), spatial_cache.reshape(rows, D), modulation, weights)
    outs = pl.pallas_call(
        functools.partial(kernel, nt, ns, batch),
        out_shape=[jax.ShapeDtypeStruct((rows, D), jnp.bfloat16)] * 3,
        in_specs=[pl.BlockSpec(memory_space=VMEM)] * len(args),
        out_specs=[pl.BlockSpec(memory_space=VMEM)] * 3,
        scratch_shapes=[
            vmem(ns, nt, block, D),
            vmem(ns, nt, block, D),
            vmem(nt, block, D),
            vmem(2, nt, depth, 3 * D // ns),
            vmem(2, nt, depth, D // ns),
            vmem(2, ns, out_chunks, D // ns // out_chunks, D),
            vmem(ns, rows // ns, D),
            vmem(ns, rows // ns, D),
            vmem(batch, ns, span // groups, D // ns * groups),
            vmem(batch, ns, span // groups, D // ns * groups),
            vmem(nt, block, D),
            vmem(nt, block, D),
            vmem(heads, batch, ns, span, HEAD_DIM),
            vmem(heads, batch, ns, span, HEAD_DIM),
            vmem(heads, batch, ns, span, LANES),
            dma((2, 3, nt)),
            dma((2, nt)),
            dma((2, 3, nt)),
            dma((2, nt)),
            dma((2, ns, out_chunks)),
            dma((2, ns, out_chunks)),
            dma((nt,)),
            dma((ns, nt)),
            dma((ns, nt)),
            dma((ns, nt)),
            dma((ns, nt)),
            dma((ns,)),
            dma((ns,)),
            dma((batch, ns)),
            dma((batch, ns)),
            dma((nt,)),
            dma((nt,)),
        ],
        cost_estimate=pl.CostEstimate(flops=6_000_000_000, bytes_accessed=20_000_000, transcendentals=4_000_000),
        compiler_params=pltpu.CompilerParams(
            collective_id=0, has_side_effects=True, vmem_limit_bytes=LIMIT
        ),
    )(*args)
    outs = pl.pallas_call(
        leave_kernel,
        grid=(2,),
        out_shape=[jax.ShapeDtypeStruct((rows, D), jnp.bfloat16)] * 3,
        in_specs=[pl.BlockSpec((rows // 2, D), lambda i: (i, 0))] * 3,
        out_specs=[pl.BlockSpec((rows // 2, D), lambda i: (i, 0))] * 3,
    )(*outs)
    return tuple(a.reshape(latent.shape) for a in outs)


def solution(mesh):
    part = P(None, "tm", "space", None)
    return jax.shard_map(
        functools.partial(shards, mesh.shape["tm"], mesh.shape["space"]),
        mesh=mesh,
        in_specs=(part, part, P(), P(None, "tm", None)),
        out_specs=(part, part, part),
        check_vma=False,
    )
```

```python
import functools

import jax
import jax.numpy as jnp
from jax import lax
from jax.experimental import pallas as pl
from jax.experimental.pallas import tpu as pltpu
from jax.sharding import PartitionSpec as P

D = 1152
HEADS = 16
HEAD_DIM = 72
LANES = 128
LOG2E = 1.4426950408889634
QUERIES = 512
MESH = pl.DeviceIdType.MESH
VMEM = pltpu.VMEM
LIMIT = 56 * 1024 * 1024


def add_gated(h, gate, branch):
    return (h.astype(jnp.float32) + gate * branch.astype(jnp.float32)).astype(jnp.bfloat16)


def modulate(h, shift, scale):
    x = h.astype(jnp.float32)
    mean = jnp.mean(x, axis=-1, keepdims=True)
    c = x - mean
    var = jnp.mean(c * c, axis=-1, keepdims=True)
    return (c * lax.rsqrt(var + 1e-06) * (1.0 + scale) + shift).astype(jnp.bfloat16)


def mod_row(mod_ref, step, attn, which):
    return mod_ref[step, attn, which : which + 1, :]


def place():
    return lax.axis_index("tm"), lax.axis_index("space")


def device(t, s):
    return {"tm": t, "space": s}


def greet(peers):
    barrier = pltpu.get_barrier_semaphore()
    for t, s in peers:
        pl.semaphore_signal(barrier, inc=1, device_id=device(t, s), device_id_type=MESH)
    pl.semaphore_wait(barrier, len(peers))


def tm_peers(nt, t, s):
    return [(lax.rem(t + k, nt), s) for k in range(1, nt)]


def space_peers(ns, t, s):
    return [(t, lax.rem(s + k, ns)) for k in range(1, ns)]


def chip_peers(ns, s):
    return [lax.rem(s + 2 * k, ns) for k in range(1, ns // 2)], s + 1 - 2 * lax.rem(s, 2)


def remote(src, dst, send, recv, t, s):
    return pltpu.make_async_remote_copy(
        src_ref=src, dst_ref=dst, send_sem=send, recv_sem=recv, device_id=device(t, s), device_id_type=MESH
    )


class Spread:
    def __init__(self, slots, send, recv, ns, t, s, chunks):
        self.slots, self.send, self.recv, self.t, self.s, self.chunks = slots, send, recv, t, s, chunks
        self.others, self.sib = chip_peers(ns, s)
        self.started = []

    def copy(self, base, i, lane, n, to):
        ref = self.slots.at[base, i]
        return remote(ref, ref, self.send.at[lane, n], self.recv.at[base, i], self.t, to)

    def push(self, base, i, lane, n, to):
        c = self.copy(base, i, lane, n, to)
        c.start()
        self.started.append(c)

    def begin(self, ready=None, first=0, last=None):
        for n, i in list(enumerate(self.chunks))[first:last]:
            if ready is not None:
                ready(i)
            for k, o in enumerate(self.others):
                self.push(self.s, i, k, n, o)
            self.push(self.s, i, len(self.others), n, self.sib)

    def forward(self):
        for n, i in enumerate(self.chunks):
            for k, o in enumerate(self.others):
                self.copy(o, i, 0, 0, self.sib).wait_recv()
                self.push(o, i, len(self.others) + 1 + k, n, self.sib)

    def finish(self):
        for i in self.chunks:
            for base in [self.sib] + [o + self.sib - self.s for o in self.others]:
                self.copy(base, i, 0, 0, self.sib).wait_recv()

    def drain(self):
        for c in self.started:
            c.wait_send()


class Gather:
    def __init__(self, slots, send, recv, nt, t, s):
        self.slots, self.send, self.recv, self.s, self.t = slots, send, recv, s, t
        self.line = nt // 2
        self.z = t // 2
        self.pair = t + 1 - 2 * lax.rem(t, 2)
        self.stage_at = 0

    def copy(self, slot, kind, to):
        ref = self.slots.at[slot]
        return remote(ref, ref, self.send.at[kind, slot], self.recv.at[slot], to, self.s)

    def each(self, d, act, arrive):
        t, z, line = self.t, self.z, self.line

        def up(slot):
            pl.when(z + 1 < line)(lambda: act(self.copy(slot, 0, t + 2)))

        def down(slot):
            pl.when(z > 0)(lambda: act(self.copy(slot, 1, t - 2)))

        if d == 0:
            up(t)
            down(t)
            act(self.copy(t, 2, self.pair))
            return

        def from_below():
            slot = t - 2 * d
            if arrive:
                self.copy(slot, 2, self.pair).wait_recv()
            up(slot)
            act(self.copy(slot, 2, self.pair))

        def from_above():
            slot = t + 2 * d
            if arrive:
                self.copy(slot, 2, self.pair).wait_recv()
            down(slot)
            act(self.copy(slot, 2, self.pair))

        pl.when(z >= d)(from_below)
        pl.when(z + d < line)(from_above)

    def stage(self):
        if self.stage_at < self.line:
            self.each(self.stage_at, lambda c: c.start(), True)
            self.stage_at += 1

    def finish(self):
        while self.stage_at < self.line:
            self.stage()
        for z in range(self.line):
            self.copy(2 * z + 1 - lax.rem(self.t, 2), 2, self.pair).wait_recv()

    def drain(self):
        for d in range(self.line):
            self.each(d, lambda c: c.wait_send(), False)


def heads_of(qkv, heads):
    out = []
    for i in range(heads):
        parts = [qkv[:, (3 * i + j) * HEAD_DIM : (3 * i + j + 1) * HEAD_DIM] for j in range(3)]
        for j in range(2):
            sq = jnp.sum(parts[j] * parts[j], axis=-1, keepdims=True)
            parts[j] = parts[j] * lax.rsqrt(sq * (1.0 / HEAD_DIM) + 1e-06)
        out.append([p.astype(jnp.bfloat16) for p in parts])
    return out


def attend(q, k, v, mask):
    scores = lax.dot_general(q, k, (((1,), (1,)), ((), ())), preferred_element_type=jnp.float32)
    expo = jnp.exp2(scores * (HEAD_DIM**-0.5 * LOG2E)).astype(jnp.bfloat16)
    if mask is not None:
        expo = expo * mask
    out = jnp.dot(expo, v, preferred_element_type=jnp.float32)
    return (out[:, :HEAD_DIM] * (1.0 / out[:, HEAD_DIM : HEAD_DIM + 1])).astype(jnp.bfloat16)


def with_ones(v):
    return jnp.concatenate([v, jnp.ones((v.shape[0], LANES - HEAD_DIM), v.dtype)], axis=-1)


def kernel(
    nt, ns, batch, lat, cache, mod, weights, block_out, new_s, new_t,
    x, x2, own, w, v, wo, mine, o, mine_s, o_s, y, back, qs, ks, vs,
    send_w, recv_w, send_v, recv_v, send_wo, recv_wo, send_a, send_x, recv_x, send_x2, recv_x2, send_o, recv_o, send_s, recv_s, send_y, recv_y,
):
    t, s = place()
    heads = HEADS // ns
    rows = x.shape[1] * x.shape[2]
    block = rows // nt
    span = rows // batch
    out_cols, in_cols = D // ns, 3 * D // ns
    depth = weights.shape[1]

    for i in range(ns):

        @pl.when(s == i)
        def _():
            for a in range(2):
                v[a, t] = weights[a, :, 3 * D + i * out_cols : 3 * D + (i + 1) * out_cols]
                w[a, t] = weights[a, :, i * in_cols : (i + 1) * in_cols]

    greet(tm_peers(nt, t, s) + space_peers(ns, t, s))
    qkv_s, qkv_t = [Gather(w.at[a], send_w.at[a], recv_w.at[a], nt, t, s) for a in range(2)]
    cols_s, cols_t = [Gather(v.at[a], send_v.at[a], recv_v.at[a], nt, t, s) for a in range(2)]
    qkv_t.stage()

    def fold(part, axis_in, axis_out):
        return jnp.concatenate(jnp.split(part, ns, axis=axis_in), axis=axis_out)

    def spread_out(a):
        wo[a, s] = fold(v[a].reshape(D, out_cols), 0, 1).reshape(wo.shape[2:])
        return Spread(wo.at[a], send_wo.at[a], recv_wo.at[a], ns, t, s, list(range(wo.shape[2])))

    h = add_gated(lat[...], mod_row(mod, 0, 0, 2), cache[...])
    block_out[...] = h
    own[...] = modulate(h, mod_row(mod, 0, 1, 0), mod_row(mod, 0, 1, 1)).reshape(own.shape)
    started = []
    for k in range(1, nt):
        p = lax.rem(t + k, nt)
        c = remote(own.at[p], x.at[s, t], send_a.at[k], recv_x.at[s, t], p, s)
        c.start()
        started.append(c)
    x[s, t] = own[t]
    qkv_t.stage()

    def ready(q):
        if q is not t:
            remote(own.at[0], x.at[s, q], send_a.at[0], recv_x.at[s, q], t, s).wait_recv()

    tokens = Spread(x, send_x, recv_x, ns, t, s, [t] + [lax.rem(t + nt - k, nt) for k in range(1, nt)])
    tokens.begin(ready, 0, nt // 2)
    qkv_t.stage()
    cols_t.stage()
    tokens.begin(ready, nt // 2, nt)
    qkv_t.stage()
    cols_t.stage()
    tokens.forward()
    qkv_t.finish()
    tokens.finish()

    mask = lax.rem(lax.broadcasted_iota(jnp.int32, (rows, rows), 0), block) == lax.rem(
        lax.broadcasted_iota(jnp.int32, (rows, rows), 1), block
    )
    mask = jnp.where(mask, 1.0, 0.0).astype(jnp.bfloat16)

    def projected(a, tokens_in):
        qkv = jnp.dot(tokens_in, w[a].reshape(nt * depth, in_cols), preferred_element_type=jnp.float32)
        return heads_of(qkv, heads)

    def send_out(step, p):
        return remote(mine.at[p], o.at[s], send_o.at[step], recv_o.at[s], t, p)

    def send_batch(b, k):
        q = lax.rem(s + k, ns)
        return remote(mine_s.at[b, q], o_s.at[b, s], send_s.at[b, k], recv_s.at[b, s], t, q)

    groups = span // mine_s.shape[2]

    def fold_rows(part):
        return jnp.concatenate(jnp.split(part, groups, axis=0), axis=1)

    def unfold_rows(part):
        return jnp.concatenate(jnp.split(part, groups, axis=1), axis=0)

    def temporal_tile(step, carry):
        p = lax.rem(s + step, ns)
        outs = [attend(q, k, with_ones(v), mask) for q, k, v in projected(1, x[p].reshape(rows, D))]
        mine[p] = fold(jnp.concatenate(outs, axis=-1), 0, 1)
        pl.when(step < ns)(lambda: send_out(step, p).start())
        pl.when(step == 1)(cols_t.stage)
        pl.when(step == 2)(lambda: (cols_t.stage(), cols_s.stage()) and None)
        return carry

    def collect():
        o[s] = mine[s]
        for k in range(1, ns):
            q = lax.rem(s + k, ns)
            remote(mine.at[q], o.at[q], send_o.at[k], recv_o.at[q], t, q).wait_recv()

    def project(a, parts):
        attn = jnp.concatenate(parts, axis=-1)
        cols = []
        for i in range(ns):
            weight = fold(wo[a, i].reshape(out_cols, D), 1, 0)
            cols.append(jnp.dot(attn, weight, preferred_element_type=jnp.float32).astype(jnp.bfloat16))
        return jnp.concatenate(cols, axis=-1)

    lax.fori_loop(1, ns + 1, temporal_tile, 0)
    cols_t.finish()
    out_t = spread_out(1)
    out_t.begin()
    cols_s.stage()
    qkv_s.stage()
    collect()
    cols_s.stage()
    out_t.forward()
    cols_s.stage()
    qkv_s.stage()
    out_t.finish()
    y[...] = project(1, [fold(o[i], 1, 0) for i in range(ns)]).reshape(y.shape)
    for k in range(1, nt):
        p = lax.rem(t + k, nt)
        c = remote(y.at[p], back.at[t], send_y.at[k], recv_y.at[t], p, s)
        c.start()
        started.append(c)
    back[t] = y[t]
    cols_s.finish()
    out_s = spread_out(0)
    out_s.begin()
    qkv_s.stage()

    def returned(q):
        if q is not t:
            remote(y.at[q], back.at[q], send_y.at[0], recv_y.at[q], t, s).wait_recv()
        at = pl.ds(pl.multiple_of(q * block, block), block)
        new_t[at, :] = back[q]
        h = add_gated(block_out[at, :], mod_row(mod, 0, 1, 2), back[q])
        block_out[at, :] = h
        x2[s, q] = modulate(h, mod_row(mod, 1, 0, 0), mod_row(mod, 1, 0, 1))

    tokens2 = Spread(x2, send_x2, recv_x2, ns, t, s, [t] + [lax.rem(t + nt - k, nt) for k in range(1, nt)])
    tokens2.begin(returned)
    qkv_s.stage()
    out_s.forward()
    tokens2.forward()
    qkv_s.finish()

    def proj(p, carry):
        p = lax.rem(s + p, ns)
        for i, (q, k, v) in enumerate(projected(0, x2[p].reshape(rows, D))):
            for b in range(batch):
                part = slice(b * span, (b + 1) * span)
                qs[i, b, p] = q[part]
                ks[i, b, p] = k[part]
                vs[i, b, p] = with_ones(v[part])
        return carry

    proj(0, 0)
    tokens2.finish()
    lax.fori_loop(1, ns, proj, 0)

    def spatial_batch(b, carry):
        total = ns * span
        step = min(QUERIES, total)
        parts = [[] for _ in range(total // step)]
        for i in range(heads):
            queries = qs[i, b].reshape(total, HEAD_DIM)
            keys = ks[i, b].reshape(total, HEAD_DIM)
            vals = vs[i, b].reshape(total, LANES)
            for j, part in enumerate(parts):
                part.append(attend(queries[j * step : (j + 1) * step], keys, vals, None))
        attn = jnp.concatenate([jnp.concatenate(part, axis=-1) for part in parts], axis=0)
        for i in range(ns):
            mine_s[b, i] = fold_rows(attn[i * span : (i + 1) * span])
        for k in range(1, ns):
            send_batch(b, k).start()
        return carry

    lax.fori_loop(0, batch, spatial_batch, 0)
    for b in range(batch):
        o_s[b, s] = mine_s[b, s]
        for k in range(1, ns):
            q = lax.rem(s + k, ns)
            remote(mine_s.at[b, q], o_s.at[b, q], send_s.at[b, k], recv_s.at[b, q], t, q).wait_recv()
    out_s.finish()
    fresh = project(0, [jnp.concatenate([unfold_rows(o_s[b, i]) for b in range(batch)], axis=0) for i in range(ns)])
    new_s[...] = fresh
    h = add_gated(block_out[...], mod_row(mod, 1, 0, 2), fresh)
    block_out[...] = add_gated(h, mod_row(mod, 1, 1, 2), new_t[...])
    for k in range(1, ns):
        send_out(k, lax.rem(s + k, ns)).wait_send()
        for b in range(batch):
            send_batch(b, k).wait_send()
    for c in started:
        c.wait_send()
    for part in [qkv_t, cols_t, qkv_s, cols_s, out_t, out_s, tokens, tokens2]:
        part.drain()


def leave_kernel(*refs):
    for i in range(3):
        refs[3 + i][...] = refs[i][...]


def shards(nt, ns, latent, spatial_cache, modulation, weights):
    batch, _, span, _ = latent.shape
    rows = batch * span
    block = rows // nt
    depth = weights.shape[1]
    heads = HEADS // ns
    dma = pltpu.SemaphoreType.DMA
    out_chunks = 2 if D // ns % 32 == 0 else 1
    groups = min(ns, span // 16)

    def vmem(*shape):
        return VMEM(shape, jnp.bfloat16)

    args = (latent.reshape(rows, D), spatial_cache.reshape(rows, D), modulation, weights)
    outs = pl.pallas_call(
        functools.partial(kernel, nt, ns, batch),
        out_shape=[jax.ShapeDtypeStruct((rows, D), jnp.bfloat16)] * 3,
        in_specs=[pl.BlockSpec(memory_space=VMEM)] * len(args),
        out_specs=[pl.BlockSpec(memory_space=VMEM)] * 3,
        scratch_shapes=[
            vmem(ns, nt, block, D),
            vmem(ns, nt, block, D),
            vmem(nt, block, D),
            vmem(2, nt, depth, 3 * D // ns),
            vmem(2, nt, depth, D // ns),
            vmem(2, ns, out_chunks, D // ns // out_chunks, D),
            vmem(ns, rows // ns, D),
            vmem(ns, rows // ns, D),
            vmem(batch, ns, span // groups, D // ns * groups),
            vmem(batch, ns, span // groups, D // ns * groups),
            vmem(nt, block, D),
            vmem(nt, block, D),
            vmem(heads, batch, ns, span, HEAD_DIM),
            vmem(heads, batch, ns, span, HEAD_DIM),
            vmem(heads, batch, ns, span, LANES),
            dma((2, 3, nt)),
            dma((2, nt)),
            dma((2, 3, nt)),
            dma((2, nt)),
            dma((2, ns, out_chunks)),
            dma((2, ns, out_chunks)),
            dma((nt,)),
            dma((ns, nt)),
            dma((ns, nt)),
            dma((ns, nt)),
            dma((ns, nt)),
            dma((ns,)),
            dma((ns,)),
            dma((batch, ns)),
            dma((batch, ns)),
            dma((nt,)),
            dma((nt,)),
        ],
        cost_estimate=pl.CostEstimate(flops=6_000_000_000, bytes_accessed=20_000_000, transcendentals=4_000_000),
        compiler_params=pltpu.CompilerParams(
            collective_id=0, has_side_effects=True, vmem_limit_bytes=LIMIT
        ),
    )(*args)
    outs = pl.pallas_call(
        leave_kernel,
        grid=(2,),
        out_shape=[jax.ShapeDtypeStruct((rows, D), jnp.bfloat16)] * 3,
        in_specs=[pl.BlockSpec((rows // 2, D), lambda i: (i, 0))] * 3,
        out_specs=[pl.BlockSpec((rows // 2, D), lambda i: (i, 0))] * 3,
    )(*outs)
    return tuple(a.reshape(latent.shape) for a in outs)


def solution(mesh):
    part = P(None, "tm", "space", None)
    return jax.shard_map(
        functools.partial(shards, mesh.shape["tm"], mesh.shape["space"]),
        mesh=mesh,
        in_specs=(part, part, P(), P(None, "tm", None)),
        out_specs=(part, part, part),
        check_vma=False,
    )
```
